32 devices in a mesh: gx: 4 (over z), gy: 4 (over y, x), gz: 2 (over core).
Axes of the slice: x: 2, y: 2, z: 4, core: 2. Of those that a mesh axis runs over, the one named last changes fastest.
Arguments:
- populations: float32 [27, 16, 64, 256], P(None, 'gx', 'gy', 'gz'), as said below
- relax: float32 [27], replicated, may hold values from 0.8 to 1.9
- entry_point: int32 [32768], P(('gx', 'gy', 'gz')), may hold values from 0 to 3599, as said below
- entry_offset: int32 [3, 32768], P(None, ('gx', 'gy', 'gz')), may hold values from -3 to 127, as said below
- entry_weight: float32 [64, 32768], P(None, ('gx', 'gy', 'gz')), may hold values from 0 to 0.04
- entry_count: int32 [32], P(('gx', 'gy', 'gz')), may hold values from 128 to 1024, as said below
- turbine_owner: int32 [4], replicated, may hold values from 0 to 3, each once
- mode_shapes: bfloat16 [4, 2700, 512], P('gx'), may hold values from -0.25 to 0.25
- coupling: float32 [4, 512, 512], P('gx')
- modal_disp: float32 [4, 512], P('gx'), may hold values from -6 to 6
- modal_vel: float32 [4, 512], P('gx'), may hold values from -0.6 to 0.6
- rigid_vel: float32 [4, 3, 900], P('gx'), may hold values from -0.9 to 0.9
- drag_coef: float32 [4, 900], P('gx'), may hold values from 200 to 2000
Outputs:
- populations_out: float32 [27, 16, 64, 256], P(None, 'gx', 'gy', 'gz')
- body_force: float32 [3, 16, 64, 256], P(None, 'gx', 'gy', 'gz')
- modal_disp_new: float32 [4, 512], P('gx')
- modal_vel_new: float32 [4, 512], P('gx')
The draws below stay inside these ranges and needn't reach their ends.
Inputs may be any that keep to these rules, and one draw needn't show every extreme that they name: `entry_point`: the live slots of one device name points of at most two turbines and at most 512 slots for each; a point id is turbine 900 + point. Live slots are the first entry_count of a device's list. `entry_offset`: row c lies from 1 - 4 to the brick's cells along dimension c less one (4, 16, 128 in turn), so every tile meets its brick. `turbine_owner`: each gx index owns exactly one turbine. All populations are positive.
All inputs are finite; a program needn't handle non-finite values.
Results may differ from the reference program's by a relative error of at most 0.0036.
Values sent between devices are 32-bit elements; how exact they have to be, the bound alone decides.
A program may use at most 64 MiB of HBM per device.

```python
import math
import jax
import jax.numpy as jnp
import numpy as np
from jax import lax

BX = 4
BY = 16
BZ = 128
LIST_CAP = 1024
MODES = 512
TILE_SIDE = 4
TILE = 64
NPT = 900
SLABS = 4
COLUMNS = 8
TURBINES = 4
ENTRIES = 32768
NX = 16
NY = 64
NZ = 256
N_GY = 4
N_GZ = 2
DEVICES = 32


def draw_populations(key, part):
    key = jax.random.fold_in(key, 21)
    pop_index = jnp.arange(27, dtype=jnp.int32)
    along_x = pop_index // 9 - 1
    along_y = pop_index // 3 % 3 - 1
    along_z = pop_index % 3 - 1
    squared = along_x * along_x + along_y * along_y + along_z * along_z
    weights = jnp.where(squared == 0, 8.0 / 27.0, jnp.where(squared == 1, 2.0 / 27.0, jnp.where(squared == 2, 1.0 / 54.0, 1.0 / 216.0))).astype(jnp.float32)
    coord_x = jnp.arange(NX, dtype=jnp.float32)[:, None, None]
    coord_y = jnp.arange(NY, dtype=jnp.float32)[None, :, None]
    coord_z = jnp.arange(NZ, dtype=jnp.float32)[None, None, :]
    wave = 2.0 * math.pi / 16.0
    pattern_one = jnp.cos(wave * (coord_x + coord_y + coord_z))
    pattern_two = jnp.cos(wave * (coord_x - coord_y + coord_z) + 1.0)
    pattern_three = jnp.sin(wave * (coord_y + coord_z - coord_x) + 2.0)
    smooth_field = jnp.exp(0.25 * (jnp.sin(math.pi * coord_x / BX + 0.7) + jnp.sin(math.pi * coord_y / BY + 1.9)) + 0.2 * jnp.sin(math.pi * coord_z / BZ + 0.4))
    noise_field = jnp.clip(jax.random.normal(key, (27, NX, NY, NZ), jnp.float32), -3.0, 3.0)
    factor_x = along_x.astype(jnp.float32)[:, None, None, None]
    factor_y = along_y.astype(jnp.float32)[:, None, None, None]
    factor_z = along_z.astype(jnp.float32)[:, None, None, None]
    drift_factor = 1.0 + 0.27 * (factor_x * pattern_one[None] + factor_y * pattern_two[None] + factor_z * pattern_three[None])
    return weights[:, None, None, None] * drift_factor * smooth_field[None] * jnp.exp(0.35 * noise_field)


def draw_entry_point(key, part):
    key = jax.random.fold_in(key, 22)
    first_key, second_key, third_key, fourth_key = jax.random.split(key, 4)
    first_turbine = jax.random.randint(first_key, (DEVICES,), 0, TURBINES, jnp.int32)
    second_turbine = (first_turbine + jax.random.randint(second_key, (DEVICES,), 1, TURBINES, jnp.int32)) % TURBINES
    position_order = jax.vmap(lambda one_key: jax.random.permutation(one_key, LIST_CAP))(jax.random.split(third_key, DEVICES))
    chosen_turbine = jnp.where(position_order < LIST_CAP // 2, first_turbine[:, None], second_turbine[:, None])
    point_local = jax.random.randint(fourth_key, (DEVICES, LIST_CAP), 0, NPT, jnp.int32)
    return (chosen_turbine * NPT + point_local).reshape(ENTRIES).astype(jnp.int32)


def draw_entry_offset(key, part):
    key = jax.random.fold_in(key, 23)
    upper_bound = jnp.array([BX, BY, BZ], jnp.int32)[:, None]
    return jax.random.randint(key, (3, ENTRIES), 1 - TILE_SIDE, upper_bound, jnp.int32)


def draw_entry_count(key, part):
    key = jax.random.fold_in(key, 24)
    first_key, second_key = jax.random.split(key, 2)
    counts = jax.random.randint(first_key, (SLABS, COLUMNS), LIST_CAP // 8, LIST_CAP // 2 + 1, jnp.int32)
    full_column = jax.random.randint(second_key, (SLABS,), 0, COLUMNS, jnp.int32)
    column_index = jnp.arange(COLUMNS, dtype=jnp.int32)
    counts = jnp.where(column_index[None, :] == full_column[:, None], LIST_CAP, counts)
    return counts.reshape(DEVICES).astype(jnp.int32)


def draw_coupling(key, part):
    key = jax.random.fold_in(key, 25)
    first_key, second_key = jax.random.split(key, 2)
    diagonal = jnp.exp(jax.random.uniform(first_key, (TURBINES, MODES), jnp.float32, jnp.log(20.0), jnp.log(100.0)))
    off_diagonal = jnp.clip(jax.random.normal(second_key, (TURBINES, MODES, MODES), jnp.float32), -4.0, 4.0)
    off_diagonal = off_diagonal * (12.0 / jnp.sqrt(jnp.float32(MODES)))
    mode_index = jnp.arange(MODES, dtype=jnp.int32)
    on_diagonal = mode_index[:, None] == mode_index[None, :]
    return jnp.where(on_diagonal[None], diagonal[:, :, None], off_diagonal).astype(jnp.float32)


def shard_levels(key, extent, cuts, least, largest):
    def one(dim, blocks):
        steps = jax.random.uniform(jax.random.fold_in(jax.random.fold_in(key, 6), dim), (blocks,), jnp.float32, least / len(cuts), largest / len(cuts))
        return jnp.repeat(jnp.exp(steps), extent[dim] // blocks).reshape((-1,) + (1,) * (len(extent) - dim - 1))

    factor_of = one(*cuts[0])
    for cut in cuts[1:]:
        factor_of = factor_of * one(*cut)
    return factor_of


def centred(stream_key, dims, scale, bound, cuts=(), kind=jnp.bfloat16):
    drawn = scale * jax.random.normal(stream_key, dims, jnp.float32)
    if cuts:
        drawn = drawn * shard_levels(stream_key, dims, cuts, -0.22, 0.18)
    return jnp.clip(drawn, -bound, bound).astype(kind)


def setup_inputs(seed: int = 0) -> dict:
    key_list = jax.random.split(jax.random.key(seed), 14)
    populations = draw_populations(jax.random.fold_in(key_list[13], 71), 0)
    relax = jnp.clip(jax.random.uniform(key_list[1], (27,), jnp.float32, 0.8, 1.9), 0.8, 1.9)
    entry_point = draw_entry_point(jax.random.fold_in(key_list[13], 71), 0)
    entry_offset = draw_entry_offset(jax.random.fold_in(key_list[13], 71), 0)
    entry_weight = jnp.clip(0.04 * jax.random.uniform(key_list[4], (TILE, ENTRIES), jnp.float32) ** shard_levels(key_list[4], (TILE, ENTRIES), ((1, 32),), -0.2, 0.2), 0.0, 0.04)
    entry_count = draw_entry_count(jax.random.fold_in(key_list[13], 71), 0)
    turbine_owner = jax.random.permutation(key_list[6], TURBINES).astype(jnp.int32)
    mode_shapes = centred(key_list[7], (TURBINES, 3 * NPT, MODES), MODES ** -0.5, 0.25, ((0, 4),))
    coupling = draw_coupling(jax.random.fold_in(key_list[13], 71), 0)
    modal_disp = centred(key_list[9], (TURBINES, MODES), 1.0, 6.0, ((0, 4),), jnp.float32)
    modal_vel = centred(key_list[10], (TURBINES, MODES), 0.1, 0.6, ((0, 4),), jnp.float32)
    rigid_vel = centred(key_list[11], (TURBINES, 3, NPT), 0.15, 0.9, ((0, 4),), jnp.float32)
    drag_coef = jnp.clip(jnp.exp(math.log(2000.0) - 2.3025851 * jax.random.uniform(key_list[12], (TURBINES, NPT), jnp.float32) ** shard_levels(key_list[12], (TURBINES, NPT), ((0, 4),), -0.2, 0.2)), 200.0, 2000.0)
    return {"populations": populations, "relax": relax, "entry_point": entry_point, "entry_offset": entry_offset, "entry_weight": entry_weight, "entry_count": entry_count, "turbine_owner": turbine_owner, "mode_shapes": mode_shapes, "coupling": coupling, "modal_disp": modal_disp, "modal_vel": modal_vel, "rigid_vel": rigid_vel, "drag_coef": drag_coef}


highest = lax.Precision.HIGHEST
inflow_speed = 0.05
force_unit = 0.02
modal_step = 0.004

def lattice_tables():
    steps_np = np.array([-1.0, 0.0, 1.0])
    along_x = np.repeat(steps_np, 9)
    along_y = np.tile(np.repeat(steps_np, 3), 3)
    along_z = np.tile(steps_np, 9)
    velocity_np = np.stack([along_x, along_y, along_z])
    squared = (along_x * along_x + along_y * along_y + along_z * along_z).astype(np.int64)
    weight_np = np.array([8.0 / 27.0, 2.0 / 27.0, 1.0 / 54.0, 1.0 / 216.0])[squared]
    vander = np.array([[1.0, 1.0, 1.0], [-1.0, 0.0, 1.0], [1.0, 0.0, 1.0]])
    inverse_one = np.array([[0.0, -0.5, 0.5], [1.0, 0.0, -1.0], [0.0, 0.5, 0.5]])
    moment_np = np.kron(np.kron(vander, vander), vander)
    inverse_np = np.kron(np.kron(inverse_one, inverse_one), inverse_one)
    return (velocity_np, weight_np, moment_np, inverse_np)

def collide(lattice_flat, momentum, density, lattice_force, relax, velocity_table, weight_table, moment_table, inverse_table):
    velocity = (momentum + 0.5 * lattice_force) / density
    along = jnp.dot(velocity_table.T, velocity, precision=highest)
    pushed = jnp.dot(velocity_table.T, lattice_force, precision=highest)
    square = lax.optimization_barrier(jnp.sum(velocity * velocity, axis=0))
    dotted = lax.optimization_barrier(jnp.sum(velocity * lattice_force, axis=0))
    weight_col = weight_table[:, None]
    equilibrium = weight_col * density * (1.0 + 3.0 * along + 4.5 * along * along - 1.5 * square)
    source = weight_col * (3.0 * (pushed - dotted) + 9.0 * along * pushed)
    relaxed = jnp.dot(inverse_table * relax[None, :], moment_table, precision=highest)
    kept = jnp.dot(inverse_table * (1.0 - 0.5 * relax)[None, :], moment_table, precision=highest)
    return lattice_flat - jnp.dot(relaxed, lattice_flat - equilibrium, precision=highest) + jnp.dot(kept, source, precision=highest)

def inflow_populations(velocity_table, weight_table):
    along = inflow_speed * velocity_table[0]
    return weight_table * (1.0 + 3.0 * along + 4.5 * along * along - 1.5 * inflow_speed * inflow_speed)

def propagate(collided, inflow, velocity_np):
    wrapped = jnp.pad(collided, ((0, 0), (1, 1), (0, 0), (0, 0)), mode='wrap')
    padded = jnp.pad(wrapped, ((0, 0), (0, 0), (1, 1), (1, 1)))
    rows_y = jnp.arange(NY + 2, dtype=jnp.int32)
    rows_z = jnp.arange(NZ + 2, dtype=jnp.int32)
    outside = ((rows_y == 0) | (rows_y == NY + 1))[:, None] | ((rows_z == 0) | (rows_z == NZ + 1))[None, :]
    padded = jnp.where(outside[None, None], inflow[:, None, None, None], padded)
    pieces = []
    for i in range(27):
        a = int(velocity_np[0, i])
        b = int(velocity_np[1, i])
        c = int(velocity_np[2, i])
        pieces.append(padded[i, 1 - a:1 - a + NX, 1 - b:1 - b + NY, 1 - c:1 - c + NZ])
    return jnp.stack(pieces)

def reference(populations, relax, entry_point, entry_offset, entry_weight, entry_count, turbine_owner, mode_shapes, coupling, modal_disp, modal_vel, rigid_vel, drag_coef):
    velocity_np, weight_np, moment_np, inverse_np = lattice_tables()
    velocity_table = jnp.asarray(velocity_np, jnp.float32)
    weight_table = jnp.asarray(weight_np, jnp.float32)
    moment_table = jnp.asarray(moment_np, jnp.float32)
    inverse_table = jnp.asarray(inverse_np, jnp.float32)
    cell_count = NX * NY * NZ
    lattice_flat = populations.reshape(27, cell_count)
    density = lax.optimization_barrier(jnp.sum(lattice_flat, axis=0))
    momentum = jnp.dot(velocity_table, lattice_flat, precision=highest)
    raw_velocity = momentum / density
    slot_number = jnp.arange(ENTRIES, dtype=jnp.int32)
    device = slot_number // LIST_CAP
    is_live = slot_number % LIST_CAP < entry_count[device]
    slab = device // COLUMNS
    column = device // N_GZ % N_GY
    layer = device % N_GZ
    tile_cells = jnp.arange(TILE, dtype=jnp.int32)
    step_x = tile_cells // (TILE_SIDE * TILE_SIDE)
    step_y = tile_cells // TILE_SIDE % TILE_SIDE
    step_z = tile_cells % TILE_SIDE
    local_x = entry_offset[0][None, :] + step_x[:, None]
    local_y = entry_offset[1][None, :] + step_y[:, None]
    local_z = entry_offset[2][None, :] + step_z[:, None]
    inside = is_live[None, :] & (local_x >= 0) & (local_x < BX) & (local_y >= 0) & (local_y < BY) & (local_z >= 0) & (local_z < BZ)
    cell_x = jnp.clip(slab[None, :] * BX + local_x, 0, NX - 1)
    cell_y = jnp.clip(column[None, :] * BY + local_y, 0, NY - 1)
    cell_z = jnp.clip(layer[None, :] * BZ + local_z, 0, NZ - 1)
    cell_index = (cell_x * NY + cell_y) * NZ + cell_z
    tile_weight = jnp.where(inside, entry_weight, 0.0)
    partial_value = lax.optimization_barrier(jnp.sum(tile_weight[None] * raw_velocity[:, cell_index], axis=1))
    turbine = entry_point // NPT
    owner_slab = turbine_owner[turbine]
    point_local = entry_point % NPT
    point_key = owner_slab * NPT + point_local
    sample = jax.ops.segment_sum(partial_value.T, point_key, num_segments=TURBINES * NPT)
    sample = sample.reshape(TURBINES, NPT, 3).transpose(0, 2, 1)
    shapes_wide = mode_shapes.astype(jnp.float32)
    vel_rounded = lax.optimization_barrier(modal_vel.astype(jnp.bfloat16)).astype(jnp.float32)
    elastic = jnp.einsum('trm,tm->tr', shapes_wide, vel_rounded, precision=highest).reshape(TURBINES, 3, NPT)
    relative = sample - rigid_vel - elastic
    rel_speed = jnp.sqrt(lax.optimization_barrier(jnp.sum(relative * relative, axis=1)))
    blade_force = drag_coef[:, None, :] * rel_speed[:, None, :] * relative
    force_rounded = lax.optimization_barrier(blade_force.reshape(TURBINES, 3 * NPT).astype(jnp.bfloat16)).astype(jnp.float32)
    modal_force = jnp.einsum('trm,tr->tm', shapes_wide, force_rounded, precision=highest)
    stiff_term = jnp.einsum('tmn,tn->tm', coupling, modal_disp, precision=highest)
    vel_new = modal_vel + modal_step * (modal_force - stiff_term)
    disp_new = modal_disp + modal_step * vel_new
    entry_force = blade_force.transpose(0, 2, 1).reshape(TURBINES * NPT, 3)[point_key]
    contribution = tile_weight[None] * entry_force.T[:, None, :]
    spread = jnp.zeros((3, cell_count), jnp.float32).at[:, cell_index.reshape(-1)].add(contribution.reshape(3, -1))
    body_force = -spread
    collided = collide(lattice_flat, momentum, density, force_unit * body_force, relax, velocity_table, weight_table, moment_table, inverse_table)
    inflow = inflow_populations(velocity_table, weight_table)
    populations_out = propagate(collided.reshape(27, NX, NY, NZ), inflow, velocity_np)
    return (populations_out, body_force.reshape(3, NX, NY, NZ), disp_new, vel_new)
```

```python
import functools

import jax
import jax.numpy as jnp
import numpy as np
from jax import lax
from jax.experimental import pallas as pl
from jax.experimental.pallas import tpu as pltpu
from jax.sharding import PartitionSpec as P

TILE_SIDE = 4
LANES = 128
CHUNK = 256
MESH = pl.DeviceIdType.MESH

highest = lax.Precision.HIGHEST
inflow_speed = 0.05
force_unit = 0.02
modal_step = 0.004

NT = (((1,), (1,)), ((), ()))
NN = (((1,), (0,)), ((), ()))


def inflow_values():
    steps = (-1.0, 0.0, 1.0)
    values = []
    for a in steps:
        for b in steps:
            for c in steps:
                weight = (8.0 / 27.0, 2.0 / 27.0, 1.0 / 54.0, 1.0 / 216.0)[
                    int(a * a + b * b + c * c)
                ]
                along = inflow_speed * a
                values.append(
                    weight
                    * (1.0 + 3.0 * along + 4.5 * along * along - 1.5 * inflow_speed * inflow_speed)
                )
    return [float(np.float32(v)) for v in values]


def transform(values, one):
    values = list(values)
    for stride in (9, 3, 1):
        for base in range(27):
            if base // stride % 3 == 0:
                spots = (base, base + stride, base + 2 * stride)
                for spot, value in zip(spots, one(*(values[s] for s in spots))):
                    values[spot] = value
    return values


def to_moments(low, mid, high):
    both = low + high
    return both + mid, high - low, both


def from_moments(zeroth, first, second):
    return 0.5 * (second - first), zeroth - second, 0.5 * (first + second)


def halves(value):
    high = value.astype(jnp.bfloat16)
    return high, (value - high.astype(jnp.float32)).astype(jnp.bfloat16)


def kernel(
    sizes,
    pops,
    relax,
    point_in,
    offset_in,
    weight_in,
    count_in,
    owner_in,
    shapes_hbm,
    stiff_in,
    disp_in,
    vel_in,
    aux_in,
    pops_out,
    force_out,
    disp_out,
    vel_out,
    shapes,
    moments,
    cells,
    raw_pair,
    pick_z,
    kern_xy,
    pick_low,
    dense,
    dense_in,
    slab_sum,
    slab_in,
    aux,
    aux_all,
    blade,
    blade_all,
    erow,
    spread,
    z_send,
    z_in,
    y_send,
    y_in,
    x_in,
    copy_sem,
    send_sem,
    recv_sem,
):
    slabs, columns, layers, points, size_x, size_y = sizes
    ranks = columns * layers
    padded = blade.shape[0] // 3
    rows = 3 * padded
    capacity = point_in.shape[1]
    plane = size_x * size_y
    gx = lax.axis_index("gx")
    gy = lax.axis_index("gy")
    gz = lax.axis_index("gz")
    rank = gy * layers + gz
    inflow = inflow_values()

    load_shapes = pltpu.make_async_copy(shapes_hbm, shapes, copy_sem)
    load_shapes.start()

    def slab_peer(step):
        return lax.rem(rank + step, ranks)

    def slab_id(other):
        return (gx, lax.div(other, layers), lax.rem(other, layers))

    def far_id(step):
        return (lax.rem(gx + step, slabs), gy, gz)

    barrier = pltpu.get_barrier_semaphore()
    for step in range(1, slabs):
        pl.semaphore_signal(barrier, inc=1, device_id=far_id(step), device_id_type=MESH)
    for step in range(1, ranks):
        pl.semaphore_signal(
            barrier, inc=1, device_id=slab_id(slab_peer(step)), device_id_type=MESH
        )

    used = [0]
    started = []

    def send(src, dst, device):
        copy = pltpu.make_async_remote_copy(
            src_ref=src,
            dst_ref=dst,
            send_sem=send_sem.at[used[0]],
            recv_sem=recv_sem.at[used[0]],
            device_id=device,
            device_id_type=MESH,
        )
        used[0] += 1
        copy.start()
        started.append(copy)
        return copy

    def moments_of(step, _):
        part = pl.ds(pl.multiple_of(step * 8, 8), 8)
        values = transform([pops[i, part, :] for i in range(27)], to_moments)
        for m in range(27):
            moments[m, part, :] = values[m]
        inverse = 1.0 / values[0]
        for c, m in enumerate((9, 3, 1)):
            raw = values[m] * inverse
            spot = pl.ds(pl.multiple_of(step * 8 + c * plane, 8), 8)
            spread[spot, :] = raw
        return 0

    lax.fori_loop(0, plane // 8, moments_of, 0)
    raw_high, raw_low = halves(spread[...])
    raw_pair[:, :LANES] = raw_high
    raw_pair[:, LANES:] = raw_low

    load_shapes.wait()
    vel8 = jnp.broadcast_to(vel_in[...], (8, vel_in.shape[1])).astype(jnp.bfloat16)
    erow[...] = jnp.zeros_like(erow)
    erow[:, : 3 * points] = lax.dot_general(
        vel8, shapes[...], NT, preferred_element_type=jnp.float32
    )
    width = erow.shape[1]
    line = erow[...]
    shifted = [
        line if c == 0 else pltpu.roll(line, width - c * points, 1) for c in range(3)
    ]
    row8 = lax.broadcasted_iota(jnp.int32, (8, LANES), 0)
    lane8 = lax.broadcasted_iota(jnp.int32, (8, LANES), 1)
    for jh in range(8):
        spot = slice(jh * LANES, (jh + 1) * LANES)
        both = jnp.where(
            row8 == 0,
            shifted[0][:, spot],
            jnp.where(row8 == 1, shifted[1][:, spot], shifted[2][:, spot]),
        )
        inside = (row8 < 3) & (lane8 + jh * LANES < points)
        aux[jh] = aux_in[jh] + jnp.where(inside, both, 0.0)
    pl.semaphore_wait(barrier, slabs - 1 + ranks - 1)
    aux_copies = [
        send(aux.at[rank], aux_all.at[gx], far_id(step)) for step in range(1, slabs)
    ]
    aux_all[gx] = aux[rank]

    dense[...] = jnp.zeros_like(dense)
    count = count_in[0]
    iota_y = lax.broadcasted_iota(jnp.int32, (size_y, CHUNK), 0)
    iota_z = lax.broadcasted_iota(jnp.int32, (LANES, CHUNK), 0)
    iota_s = lax.broadcasted_iota(jnp.int32, (padded, CHUNK), 0)
    iota_r = lax.broadcasted_iota(jnp.int32, (1, CHUNK), 1)

    def slots_of(part):
        name = point_in[:, part]
        turbine = jnp.zeros_like(name)
        for t in range(1, slabs):
            turbine = turbine + jnp.where(name >= t * points, 1, 0)
        owner = jnp.zeros_like(name)
        for t in range(slabs):
            owner = owner + jnp.where(turbine == t, owner_in[t], 0)
        point = name - turbine * points
        high = lax.shift_right_logical(point, 7)
        masks = [(iota_s == owner) & (high == jh) for jh in range(8)]
        return point - high * LANES, masks

    def gather(step, _):
        base = pl.multiple_of(step * CHUNK, CHUNK)
        part = pl.ds(base, CHUNK)
        weight = jnp.where(iota_r + base < count, weight_in[:, part], 0.0)
        off_x = offset_in[0:1, part]
        off_y = offset_in[1:2, part]
        off_z = offset_in[2:3, part]
        at_y = [off_y + b == iota_y for b in range(TILE_SIDE)]
        by_x = []
        for x in range(size_x):
            value = jnp.zeros((16, CHUNK), jnp.float32)
            for a in range(TILE_SIDE):
                value = jnp.where(off_x + a == x, weight[16 * a : 16 * a + 16], value)
            by_x.append(value)
        total = [jnp.zeros((size_y, CHUNK), jnp.float32) for _ in range(3)]
        for c in range(TILE_SIDE):
            at_z = jnp.where(off_z + c == iota_z, 1.0, 0.0).astype(jnp.bfloat16)
            pick_z[c, :, part] = at_z
            layer = lax.dot_general(
                raw_pair[...],
                jnp.concatenate([at_z, at_z], axis=0),
                NN,
                preferred_element_type=jnp.float32,
            )
            for x in range(size_x):
                value = jnp.zeros((size_y, CHUNK), jnp.float32)
                for b in range(TILE_SIDE):
                    row = 4 * b + c
                    value = jnp.where(at_y[b], by_x[x][row : row + 1], value)
                kern_xy[c, x * size_y : (x + 1) * size_y, part] = value
                for d in range(3):
                    first = d * plane + x * size_y
                    total[d] = total[d] + value * layer[first : first + size_y]
        partial = [jnp.sum(t, axis=0, keepdims=True) for t in total]
        low, masks = slots_of(part)
        at_low = jnp.where(low == iota_z, 1.0, 0.0).astype(jnp.bfloat16)
        pick_low[:, part] = at_low
        placed = jnp.concatenate(
            [jnp.where(masks[jh], partial[d], 0.0) for jh in range(8) for d in range(3)], axis=0
        )
        high_part, low_part = halves(placed)
        dense[...] += (
            lax.dot_general(high_part, at_low, NT, preferred_element_type=jnp.float32)
            + lax.dot_general(low_part, at_low, NT, preferred_element_type=jnp.float32)
        ).reshape(8, rows, LANES)
        return 0

    lax.fori_loop(0, capacity // CHUNK, gather, 0)

    first_copies = [
        send(dense.at[slab_peer(step)], dense_in.at[step - 1], slab_id(slab_peer(step)))
        for step in range(1, ranks)
    ]
    own = dense[rank]
    for step in range(1, ranks):
        first_copies[step - 1].wait_recv()
        own = own + dense_in[step - 1]
    slab_sum[...] = own
    second_copies = [
        send(slab_sum, slab_in.at[step - 1], far_id(step)) for step in range(1, slabs)
    ]
    for copy in aux_copies:
        copy.wait_recv()
    for step in range(1, slabs):
        second_copies[step - 1].wait_recv()
        own = own + slab_in[step - 1]

    blade[...] = jnp.zeros_like(blade)
    for s in range(slabs):
        here = aux_all[s]
        relative = [
            own[d * padded + s : d * padded + s + 1] - here[d : d + 1] for d in range(3)
        ]
        speed = jnp.sqrt(
            relative[0] * relative[0] + relative[1] * relative[1] + relative[2] * relative[2]
        )
        factor = here[3:4] * speed
        for d in range(3):
            spot = d * padded + s
            blade[spot : spot + 1, :] = factor * relative[d]
    blade_all[rank] = blade[...]
    third_copies = [
        send(blade, blade_all.at[rank], slab_id(slab_peer(step))) for step in range(1, ranks)
    ]
    for copy in third_copies:
        copy.wait_recv()

    blade_high, blade_low = halves(blade_all[...].reshape(8 * rows, LANES))
    blade_pair = jnp.concatenate([blade_high, blade_low], axis=1)
    spread[...] = jnp.zeros_like(spread)

    def scatter(step, _):
        part = pl.ds(pl.multiple_of(step * CHUNK, CHUNK), CHUNK)
        _, masks = slots_of(part)
        at_low = pick_low[:, part]
        found = lax.dot_general(
            blade_pair,
            jnp.concatenate([at_low, at_low], axis=0),
            NN,
            preferred_element_type=jnp.float32,
        )
        forces = []
        for d in range(3):
            value = jnp.zeros((padded, CHUNK), jnp.float32)
            for jh in range(8):
                first = jh * rows + d * padded
                value = jnp.where(masks[jh], found[first : first + padded], value)
            forces.append(jnp.sum(value, axis=0, keepdims=True))
        total = jnp.zeros(spread.shape, jnp.float32)
        for c in range(TILE_SIDE):
            kern = kern_xy[c, :, part]
            high_part, low_part = halves(
                jnp.concatenate([kern * forces[d] for d in range(3)], axis=0)
            )
            at_z = pick_z[c, :, part]
            total = total + (
                lax.dot_general(high_part, at_z, NT, preferred_element_type=jnp.float32)
                + lax.dot_general(low_part, at_z, NT, preferred_element_type=jnp.float32)
            )
        spread[...] += total
        return 0

    lax.fori_loop(0, capacity // CHUNK, scatter, 0)
    force_out[...] = -spread[...]

    def collide(step, _):
        part = pl.ds(pl.multiple_of(step * 8, 8), 8)
        density = moments[0, part, :]
        inverse = 1.0 / density
        force = [
            force_unit * force_out[pl.ds(pl.multiple_of(step * 8 + d * plane, 8), 8), :]
            for d in range(3)
        ]
        velocity = [
            (moments[m, part, :] + 0.5 * force[d]) * inverse for d, m in enumerate((9, 3, 1))
        ]
        pushed = [density * v for v in velocity]
        pairs = {}
        sources = {}
        for d in range(3):
            for e in range(d, 3):
                pairs[d, e] = pushed[d] * velocity[e]
                sources[d, e] = velocity[d] * force[e] + velocity[e] * force[d]
        values = []
        for m in range(27):
            powers = (m // 9, m // 3 % 3, m % 3)
            odd = [d for d in range(3) if powers[d] == 1]
            even = [d for d in range(3) if powers[d] == 2]
            scale = (1.0 / 3.0) ** len(even)
            source = None
            if len(odd) == 0:
                wanted = density * scale
                if even:
                    square = pairs[even[0], even[0]]
                    source = sources[even[0], even[0]]
                    for d in even[1:]:
                        square = square + pairs[d, d]
                        source = source + sources[d, d]
                    wanted = wanted + square * (3.0 * scale)
                    source = source * (3.0 * scale)
            elif len(odd) == 1:
                wanted = pushed[odd[0]] * scale
                source = force[odd[0]] * scale
            elif len(odd) == 2:
                wanted = pairs[odd[0], odd[1]] * scale
                source = sources[odd[0], odd[1]] * scale
            else:
                wanted = None
            rate = relax[m]
            here = moments[m, part, :]
            gap = here if wanted is None else here - wanted
            value = -rate * gap
            if source is not None:
                value = value + (1.0 - 0.5 * rate) * source
            values.append(value)
        values = transform(values, from_moments)
        for i in range(27):
            cells[i, part, :] = pops[i, part, :] + values[i]
        return 0

    lax.fori_loop(0, plane // 8, collide, 0)

    lane = lax.broadcasted_iota(jnp.int32, (plane, LANES), 1)
    at_bottom = gz == 0
    packed = jnp.zeros((plane, LANES), jnp.float32)
    for k in range(9):
        column = jnp.where(
            at_bottom,
            pltpu.roll(cells[3 * k + 2], k + 1, 1),
            cells[3 * k] if k == 0 else pltpu.roll(cells[3 * k], k, 1),
        )
        packed = jnp.where(lane == k, column, packed)
    z_send[...] = packed
    z_copy = send(z_send, z_in, (gx, gy, 1 - gz))

    pieces = []
    for d in range(3):
        chunks = [
            jnp.broadcast_to(blade_all[jh, pl.ds(d * padded + gx, 1), :], (8, LANES))
            for jh in range(8)
        ]
        chunks.append(jnp.zeros((8, width - 8 * LANES), jnp.float32))
        piece = jnp.concatenate(chunks, axis=1)
        pieces.append(piece if d == 0 else pltpu.roll(piece, d * points, 1))
    erow[...] = pieces[0] + pieces[1] + pieces[2]
    modal = lax.dot_general(
        erow[:, : 3 * points].astype(jnp.bfloat16),
        shapes[...],
        NN,
        preferred_element_type=jnp.float32,
    )[0:1]
    vel_new = vel_in[...] + modal_step * (modal - stiff_in[...])
    vel_out[...] = vel_new
    disp_out[...] = disp_in[...] + modal_step * vel_new

    z_copy.wait_recv()
    column = z_in[...]
    for k in range(9):
        up, down = 3 * k + 2, 3 * k
        above = column if k == 0 else pltpu.roll(column, LANES - k, 1)
        cells[up] = jnp.where(
            lane == 0, jnp.where(at_bottom, inflow[up], above), pltpu.roll(cells[up], 1, 1)
        )
        cells[down] = jnp.where(
            lane == LANES - 1,
            jnp.where(at_bottom, pltpu.roll(column, LANES - 1 - k, 1), inflow[down]),
            pltpu.roll(cells[down], LANES - 1, 1),
        )

    ups = [i for i in range(27) if i // 3 % 3 == 2]
    downs = [i for i in range(27) if i // 3 % 3 == 0]
    for k in range(9):
        for x in range(size_x):
            spot = k * size_x + x
            last = (x + 1) * size_y - 1
            y_send[0, spot : spot + 1, :] = cells[ups[k], last : last + 1, :]
            first = x * size_y
            y_send[1, spot : spot + 1, :] = cells[downs[k], first : first + 1, :]
    y_copies = [
        send(y_send.at[0], y_in.at[0], (gx, lax.rem(gy + 1, columns), gz)),
        send(y_send.at[1], y_in.at[1], (gx, lax.rem(gy + columns - 1, columns), gz)),
    ]
    row = lax.broadcasted_iota(jnp.int32, (size_y, LANES), 0)
    for copy in y_copies:
        copy.wait_recv()
    for k in range(9):
        for x in range(size_x):
            spot = k * size_x + x
            span = slice(x * size_y, (x + 1) * size_y)
            up, down = ups[k], downs[k]
            below = jnp.where(gy == 0, inflow[up], y_in[0, spot : spot + 1, :])
            cells[up, span, :] = jnp.where(row == 0, below, pltpu.roll(cells[up, span, :], 1, 0))
            above = jnp.where(gy == columns - 1, inflow[down], y_in[1, spot : spot + 1, :])
            cells[down, span, :] = jnp.where(
                row == size_y - 1, above, pltpu.roll(cells[down, span, :], size_y - 1, 0)
            )

    tail = plane - size_y
    x_copies = [
        send(cells.at[pl.ds(18, 9), pl.ds(tail, size_y)], x_in.at[0], far_id(1)),
        send(cells.at[pl.ds(0, 9), pl.ds(0, size_y)], x_in.at[1], far_id(slabs - 1)),
    ]
    pops_out[9:18] = cells[9:18]
    pops_out[18:27, size_y:, :] = cells[18:27, :tail, :]
    pops_out[0:9, :tail, :] = cells[0:9, size_y:, :]
    for copy in x_copies:
        copy.wait_recv()
    pops_out[18:27, :size_y, :] = x_in[0]
    pops_out[0:9, tail:, :] = x_in[1]
    for copy in started:
        copy.wait_send()


def body(
    sizes,
    populations,
    relax,
    entry_point,
    entry_offset,
    entry_weight,
    entry_count,
    turbine_owner,
    mode_shapes,
    coupling,
    modal_disp,
    modal_vel,
    rigid_vel,
    drag_coef,
):
    slabs, columns, layers = sizes
    _, size_x, size_y, size_z = populations.shape
    points = drag_coef.shape[1]
    modes = modal_vel.shape[1]
    capacity = entry_point.shape[0]
    plane = size_x * size_y
    padded = -(-slabs // 8) * 8
    rows = 3 * padded
    ranks = columns * layers
    width = -(-3 * points // LANES) * LANES
    assert ranks == 8 and layers == 2 and size_z == LANES and points <= 8 * LANES
    stiff = jnp.dot(coupling[0], modal_disp[0], precision=highest)[None, :]
    aux = jnp.concatenate([rigid_vel[0], drag_coef], axis=0)
    aux = jnp.pad(aux, ((0, 4), (0, 8 * LANES - points)))
    aux = aux.reshape(8, 8, LANES).transpose(1, 0, 2)
    copies = 2 * (slabs - 1) + 2 * (ranks - 1) + 5
    vmem = pl.BlockSpec(memory_space=pltpu.VMEM)
    smem = pl.BlockSpec(memory_space=pltpu.SMEM)
    full = jnp.float32
    half = jnp.bfloat16
    out = pl.pallas_call(
        functools.partial(kernel, (slabs, columns, layers, points, size_x, size_y)),
        out_shape=(
            jax.ShapeDtypeStruct((27, plane, size_z), full),
            jax.ShapeDtypeStruct((3 * plane, size_z), full),
            jax.ShapeDtypeStruct((1, modes), full),
            jax.ShapeDtypeStruct((1, modes), full),
        ),
        in_specs=[vmem, smem, vmem, vmem, vmem, smem, smem, pl.BlockSpec(memory_space=pl.ANY)]
        + [vmem] * 4,
        out_specs=(vmem,) * 4,
        scratch_shapes=[
            pltpu.VMEM((3 * points, modes), half),
            pltpu.VMEM((27, plane, size_z), full),
            pltpu.VMEM((27, plane, size_z), full),
            pltpu.VMEM((3 * plane, 2 * LANES), half),
            pltpu.VMEM((TILE_SIDE, LANES, capacity), half),
            pltpu.VMEM((TILE_SIDE, plane, capacity), full),
            pltpu.VMEM((LANES, capacity), half),
            pltpu.VMEM((8, rows, LANES), full),
            pltpu.VMEM((ranks - 1, rows, LANES), full),
            pltpu.VMEM((rows, LANES), full),
            pltpu.VMEM((slabs - 1, rows, LANES), full),
            pltpu.VMEM((8, 8, LANES), full),
            pltpu.VMEM((slabs, 8, LANES), full),
            pltpu.VMEM((rows, LANES), full),
            pltpu.VMEM((8, rows, LANES), full),
            pltpu.VMEM((8, width), full),
            pltpu.VMEM((3 * plane, LANES), full),
            pltpu.VMEM((plane, LANES), full),
            pltpu.VMEM((plane, LANES), full),
            pltpu.VMEM((2, 9 * size_x + 4, LANES), full),
            pltpu.VMEM((2, 9 * size_x + 4, LANES), full),
            pltpu.VMEM((2, 9, size_y, LANES), full),
            pltpu.SemaphoreType.DMA,
            pltpu.SemaphoreType.DMA((copies,)),
            pltpu.SemaphoreType.DMA((copies,)),
        ],
        compiler_params=pltpu.CompilerParams(
            collective_id=0, has_side_effects=True, vmem_limit_bytes=40 * 1024 * 1024
        ),
    )(
        populations.reshape(27, plane, size_z),
        relax,
        entry_point[None, :],
        entry_offset,
        entry_weight,
        entry_count,
        turbine_owner,
        mode_shapes[0],
        stiff,
        modal_disp,
        modal_vel,
        aux,
    )
    populations_out, body_force, disp_new, vel_new = out
    return (
        populations_out.reshape(populations.shape),
        body_force.reshape(3, size_x, size_y, size_z),
        disp_new,
        vel_new,
    )


def solution(mesh):
    sizes = (mesh.shape["gx"], mesh.shape["gy"], mesh.shape["gz"])
    return jax.shard_map(
        functools.partial(body, sizes),
        mesh=mesh,
        in_specs=(
            P(None, "gx", "gy", "gz"),
            P(),
            P(("gx", "gy", "gz")),
            P(None, ("gx", "gy", "gz")),
            P(None, ("gx", "gy", "gz")),
            P(("gx", "gy", "gz")),
            P(),
            P("gx", None, None),
            P("gx", None, None),
            P("gx", None),
            P("gx", None),
            P("gx", None, None),
            P("gx", None),
        ),
        out_specs=(
            P(None, "gx", "gy", "gz"),
            P(None, "gx", "gy", "gz"),
            P("gx", None),
            P("gx", None),
        ),
        check_vma=False,
    )
```

```python
import functools

import jax
import jax.numpy as jnp
import numpy as np
from jax import lax
from jax.experimental import pallas as pl
from jax.experimental.pallas import tpu as pltpu
from jax.sharding import PartitionSpec as P

TILE_SIDE = 4
LANES = 128
CHUNK = 256
VMEM_BYTES = 64 * 1024 * 1024
MESH = pl.DeviceIdType.MESH

highest = lax.Precision.HIGHEST
inflow_speed = 0.05
force_unit = 0.02
modal_step = 0.004

NT = (((1,), (1,)), ((), ()))
NN = (((1,), (0,)), ((), ()))


def inflow_values():
    steps = (-1.0, 0.0, 1.0)
    values = []
    for a in steps:
        for b in steps:
            for c in steps:
                weight = (8.0 / 27.0, 2.0 / 27.0, 1.0 / 54.0, 1.0 / 216.0)[
                    int(a * a + b * b + c * c)
                ]
                along = inflow_speed * a
                values.append(
                    weight
                    * (1.0 + 3.0 * along + 4.5 * along * along - 1.5 * inflow_speed * inflow_speed)
                )
    return [float(np.float32(v)) for v in values]


def transform(values, one):
    values = list(values)
    for stride in (9, 3, 1):
        for base in range(27):
            if base // stride % 3 == 0:
                spots = (base, base + stride, base + 2 * stride)
                for spot, value in zip(spots, one(*(values[s] for s in spots))):
                    values[spot] = value
    return values


def to_moments(low, mid, high):
    both = low + high
    return both + mid, high - low, both


def from_moments(zeroth, first, second):
    return 0.5 * (second - first), zeroth - second, 0.5 * (first + second)


def halves(value):
    high = value.astype(jnp.bfloat16)
    return high, (value - high.astype(jnp.float32)).astype(jnp.bfloat16)


def kernel(
    sizes,
    pops_hbm,
    relax_hbm,
    point_hbm,
    offset_hbm,
    weight_hbm,
    count_hbm,
    owner_hbm,
    shapes_hbm,
    coupling_hbm,
    disp_hbm,
    vel_hbm,
    rigid_hbm,
    drag_hbm,
    pops_out,
    force_out,
    disp_out,
    vel_out,
    pops,
    relax,
    point_in,
    offset_in,
    weight_in,
    count_in,
    owner_in,
    shapes,
    coupling,
    disp_in,
    vel_in,
    rigid_in,
    drag_in,
    aux_in,
    moments,
    cells,
    raw_pair,
    pick_z,
    kern_xy,
    pick_low,
    dense,
    dense_in,
    slab_sum,
    slab_in,
    aux,
    aux_all,
    blade,
    blade_all,
    erow,
    spread,
    z_send,
    z_in,
    y_send,
    y_in,
    x_in,
    copy_sem,
    send_sem,
    recv_sem,
):
    slabs, columns, layers, points, size_x, size_y = sizes
    ranks = columns * layers
    padded = blade.shape[0] // 3
    rows = 3 * padded
    capacity = point_in.shape[1]
    plane = size_x * size_y
    gx = lax.axis_index("gx")
    gy = lax.axis_index("gy")
    gz = lax.axis_index("gz")
    rank = gy * layers + gz
    inflow = inflow_values()

    loads = {}
    for number, (name, src, dst) in enumerate(
        (
            ("pops", pops_hbm, pops),
            ("vel", vel_hbm, vel_in),
            ("rigid", rigid_hbm, rigid_in),
            ("drag", drag_hbm, drag_in),
            ("shapes", shapes_hbm, shapes),
            ("count", count_hbm, count_in),
            ("owner", owner_hbm, owner_in),
            ("point", point_hbm, point_in),
            ("offset", offset_hbm, offset_in),
            ("weight", weight_hbm, weight_in),
            ("relax", relax_hbm, relax),
            ("disp", disp_hbm, disp_in),
            ("coupling", coupling_hbm, coupling),
        )
    ):
        loads[name] = pltpu.make_async_copy(src, dst, copy_sem.at[number])
        loads[name].start()

    def slab_peer(step):
        return lax.rem(rank + step, ranks)

    def slab_id(other):
        return (gx, lax.div(other, layers), lax.rem(other, layers))

    def far_id(step):
        return (lax.rem(gx + step, slabs), gy, gz)

    barrier = pltpu.get_barrier_semaphore()
    for step in range(1, slabs):
        pl.semaphore_signal(barrier, inc=1, device_id=far_id(step), device_id_type=MESH)
    for step in range(1, ranks):
        pl.semaphore_signal(
            barrier, inc=1, device_id=slab_id(slab_peer(step)), device_id_type=MESH
        )

    used = [0]
    started = []

    def send(src, dst, device):
        copy = pltpu.make_async_remote_copy(
            src_ref=src,
            dst_ref=dst,
            send_sem=send_sem.at[used[0]],
            recv_sem=recv_sem.at[used[0]],
            device_id=device,
            device_id_type=MESH,
        )
        used[0] += 1
        copy.start()
        started.append(copy)
        return copy

    loads["pops"].wait()

    def moments_of(step, _):
        part = pl.ds(pl.multiple_of(step * 8, 8), 8)
        values = transform([pops[i, part, :] for i in range(27)], to_moments)
        for m in range(27):
            moments[m, part, :] = values[m]
        inverse = 1.0 / values[0]
        for c, m in enumerate((9, 3, 1)):
            raw = values[m] * inverse
            spot = pl.ds(pl.multiple_of(step * 8 + c * plane, 8), 8)
            spread[spot, :] = raw
        return 0

    lax.fori_loop(0, plane // 8, moments_of, 0)
    raw_high, raw_low = halves(spread[...])
    raw_pair[:, :LANES] = raw_high
    raw_pair[:, LANES:] = raw_low

    for name in ("vel", "rigid", "drag", "shapes"):
        loads[name].wait()
    aux_in[...] = jnp.zeros_like(aux_in)
    for d in range(3):
        aux_in[d : d + 1, :points] = rigid_in[d]
    aux_in[3:4, :points] = drag_in[...]
    vel8 = jnp.broadcast_to(vel_in[...], (8, vel_in.shape[1])).astype(jnp.bfloat16)
    erow[...] = jnp.zeros_like(erow)
    erow[:, : 3 * points] = lax.dot_general(
        vel8, shapes[...], NT, preferred_element_type=jnp.float32
    )
    width = erow.shape[1]
    line = erow[...]
    shifted = [
        line if c == 0 else pltpu.roll(line, width - c * points, 1) for c in range(3)
    ]
    row8 = lax.broadcasted_iota(jnp.int32, (8, LANES), 0)
    lane8 = lax.broadcasted_iota(jnp.int32, (8, LANES), 1)
    for jh in range(8):
        spot = slice(jh * LANES, (jh + 1) * LANES)
        both = jnp.where(
            row8 == 0,
            shifted[0][:, spot],
            jnp.where(row8 == 1, shifted[1][:, spot], shifted[2][:, spot]),
        )
        inside = (row8 < 3) & (lane8 + jh * LANES < points)
        aux[jh] = aux_in[:, spot] + jnp.where(inside, both, 0.0)
    pl.semaphore_wait(barrier, slabs - 1 + ranks - 1)
    aux_copies = [
        send(aux.at[rank], aux_all.at[gx], far_id(step)) for step in range(1, slabs)
    ]
    aux_all[gx] = aux[rank]

    for name in ("count", "owner", "point", "offset", "weight"):
        loads[name].wait()
    dense[...] = jnp.zeros_like(dense)
    count = count_in[0]
    iota_y = lax.broadcasted_iota(jnp.int32, (size_y, CHUNK), 0)
    iota_z = lax.broadcasted_iota(jnp.int32, (LANES, CHUNK), 0)
    iota_s = lax.broadcasted_iota(jnp.int32, (padded, CHUNK), 0)
    iota_r = lax.broadcasted_iota(jnp.int32, (1, CHUNK), 1)

    def slots_of(part):
        name = point_in[:, part]
        turbine = jnp.zeros_like(name)
        for t in range(1, slabs):
            turbine = turbine + jnp.where(name >= t * points, 1, 0)
        owner = jnp.zeros_like(name)
        for t in range(slabs):
            owner = owner + jnp.where(turbine == t, owner_in[t], 0)
        point = name - turbine * points
        high = lax.shift_right_logical(point, 7)
        masks = [(iota_s == owner) & (high == jh) for jh in range(8)]
        return point - high * LANES, masks

    def gather(step, _):
        base = pl.multiple_of(step * CHUNK, CHUNK)
        part = pl.ds(base, CHUNK)
        weight = jnp.where(iota_r + base < count, weight_in[:, part], 0.0)
        off_x = offset_in[0:1, part]
        off_y = offset_in[1:2, part]
        off_z = offset_in[2:3, part]
        at_y = [off_y + b == iota_y for b in range(TILE_SIDE)]
        by_x = []
        for x in range(size_x):
            value = jnp.zeros((16, CHUNK), jnp.float32)
            for a in range(TILE_SIDE):
                value = jnp.where(off_x + a == x, weight[16 * a : 16 * a + 16], value)
            by_x.append(value)
        total = [jnp.zeros((size_y, CHUNK), jnp.float32) for _ in range(3)]
        for c in range(TILE_SIDE):
            at_z = jnp.where(off_z + c == iota_z, 1.0, 0.0).astype(jnp.bfloat16)
            pick_z[c, :, part] = at_z
            layer = lax.dot_general(
                raw_pair[...],
                jnp.concatenate([at_z, at_z], axis=0),
                NN,
                preferred_element_type=jnp.float32,
            )
            for x in range(size_x):
                value = jnp.zeros((size_y, CHUNK), jnp.float32)
                for b in range(TILE_SIDE):
                    row = 4 * b + c
                    value = jnp.where(at_y[b], by_x[x][row : row + 1], value)
                kern_xy[c, x * size_y : (x + 1) * size_y, part] = value
                for d in range(3):
                    first = d * plane + x * size_y
                    total[d] = total[d] + value * layer[first : first + size_y]
        partial = [jnp.sum(t, axis=0, keepdims=True) for t in total]
        low, masks = slots_of(part)
        at_low = jnp.where(low == iota_z, 1.0, 0.0).astype(jnp.bfloat16)
        pick_low[:, part] = at_low
        placed = jnp.concatenate(
            [jnp.where(masks[jh], partial[d], 0.0) for jh in range(8) for d in range(3)], axis=0
        )
        high_part, low_part = halves(placed)
        dense[...] += (
            lax.dot_general(high_part, at_low, NT, preferred_element_type=jnp.float32)
            + lax.dot_general(low_part, at_low, NT, preferred_element_type=jnp.float32)
        ).reshape(8, rows, LANES)
        return 0

    lax.fori_loop(0, capacity // CHUNK, gather, 0)

    first_copies = [
        send(dense.at[slab_peer(step)], dense_in.at[step - 1], slab_id(slab_peer(step)))
        for step in range(1, ranks)
    ]
    own = dense[rank]
    for step in range(1, ranks):
        first_copies[step - 1].wait_recv()
        own = own + dense_in[step - 1]
    slab_sum[...] = own
    second_copies = [
        send(slab_sum, slab_in.at[step - 1], far_id(step)) for step in range(1, slabs)
    ]
    for copy in aux_copies:
        copy.wait_recv()
    for step in range(1, slabs):
        second_copies[step - 1].wait_recv()
        own = own + slab_in[step - 1]

    blade[...] = jnp.zeros_like(blade)
    for s in range(slabs):
        here = aux_all[s]
        relative = [
            own[d * padded + s : d * padded + s + 1] - here[d : d + 1] for d in range(3)
        ]
        speed = jnp.sqrt(
            relative[0] * relative[0] + relative[1] * relative[1] + relative[2] * relative[2]
        )
        factor = here[3:4] * speed
        for d in range(3):
            spot = d * padded + s
            blade[spot : spot + 1, :] = factor * relative[d]
    blade_all[rank] = blade[...]
    third_copies = [
        send(blade, blade_all.at[rank], slab_id(slab_peer(step))) for step in range(1, ranks)
    ]
    for copy in third_copies:
        copy.wait_recv()

    blade_high, blade_low = halves(blade_all[...].reshape(8 * rows, LANES))
    blade_pair = jnp.concatenate([blade_high, blade_low], axis=1)
    spread[...] = jnp.zeros_like(spread)

    def scatter(step, _):
        part = pl.ds(pl.multiple_of(step * CHUNK, CHUNK), CHUNK)
        _, masks = slots_of(part)
        at_low = pick_low[:, part]
        found = lax.dot_general(
            blade_pair,
            jnp.concatenate([at_low, at_low], axis=0),
            NN,
            preferred_element_type=jnp.float32,
        )
        forces = []
        for d in range(3):
            value = jnp.zeros((padded, CHUNK), jnp.float32)
            for jh in range(8):
                first = jh * rows + d * padded
                value = jnp.where(masks[jh], found[first : first + padded], value)
            forces.append(jnp.sum(value, axis=0, keepdims=True))
        total = jnp.zeros(spread.shape, jnp.float32)
        for c in range(TILE_SIDE):
            kern = kern_xy[c, :, part]
            high_part, low_part = halves(
                jnp.concatenate([kern * forces[d] for d in range(3)], axis=0)
            )
            at_z = pick_z[c, :, part]
            total = total + (
                lax.dot_general(high_part, at_z, NT, preferred_element_type=jnp.float32)
                + lax.dot_general(low_part, at_z, NT, preferred_element_type=jnp.float32)
            )
        spread[...] += total
        return 0

    lax.fori_loop(0, capacity // CHUNK, scatter, 0)
    force_out[...] = -spread[...]

    loads["relax"].wait()

    def collide(step, _):
        part = pl.ds(pl.multiple_of(step * 8, 8), 8)
        density = moments[0, part, :]
        inverse = 1.0 / density
        force = [
            force_unit * force_out[pl.ds(pl.multiple_of(step * 8 + d * plane, 8), 8), :]
            for d in range(3)
        ]
        velocity = [
            (moments[m, part, :] + 0.5 * force[d]) * inverse for d, m in enumerate((9, 3, 1))
        ]
        pushed = [density * v for v in velocity]
        pairs = {}
        sources = {}
        for d in range(3):
            for e in range(d, 3):
                pairs[d, e] = pushed[d] * velocity[e]
                sources[d, e] = velocity[d] * force[e] + velocity[e] * force[d]
        values = []
        for m in range(27):
            powers = (m // 9, m // 3 % 3, m % 3)
            odd = [d for d in range(3) if powers[d] == 1]
            even = [d for d in range(3) if powers[d] == 2]
            scale = (1.0 / 3.0) ** len(even)
            source = None
            if len(odd) == 0:
                wanted = density * scale
                if even:
                    square = pairs[even[0], even[0]]
                    source = sources[even[0], even[0]]
                    for d in even[1:]:
                        square = square + pairs[d, d]
                        source = source + sources[d, d]
                    wanted = wanted + square * (3.0 * scale)
                    source = source * (3.0 * scale)
            elif len(odd) == 1:
                wanted = pushed[odd[0]] * scale
                source = force[odd[0]] * scale
            elif len(odd) == 2:
                wanted = pairs[odd[0], odd[1]] * scale
                source = sources[odd[0], odd[1]] * scale
            else:
                wanted = None
            rate = relax[m]
            here = moments[m, part, :]
            gap = here if wanted is None else here - wanted
            value = -rate * gap
            if source is not None:
                value = value + (1.0 - 0.5 * rate) * source
            values.append(value)
        values = transform(values, from_moments)
        for i in range(27):
            cells[i, part, :] = pops[i, part, :] + values[i]
        return 0

    lax.fori_loop(0, plane // 8, collide, 0)

    lane = lax.broadcasted_iota(jnp.int32, (plane, LANES), 1)
    at_bottom = gz == 0
    packed = jnp.zeros((plane, LANES), jnp.float32)
    for k in range(9):
        column = jnp.where(
            at_bottom,
            pltpu.roll(cells[3 * k + 2], k + 1, 1),
            cells[3 * k] if k == 0 else pltpu.roll(cells[3 * k], k, 1),
        )
        packed = jnp.where(lane == k, column, packed)
    z_send[...] = packed
    z_copy = send(z_send, z_in, (gx, gy, 1 - gz))

    pieces = []
    for d in range(3):
        chunks = [
            jnp.broadcast_to(blade_all[jh, pl.ds(d * padded + gx, 1), :], (8, LANES))
            for jh in range(8)
        ]
        chunks.append(jnp.zeros((8, width - 8 * LANES), jnp.float32))
        piece = jnp.concatenate(chunks, axis=1)
        pieces.append(piece if d == 0 else pltpu.roll(piece, d * points, 1))
    erow[...] = pieces[0] + pieces[1] + pieces[2]
    modal = lax.dot_general(
        erow[:, : 3 * points].astype(jnp.bfloat16),
        shapes[...],
        NN,
        preferred_element_type=jnp.float32,
    )[0:1]
    loads["disp"].wait()
    loads["coupling"].wait()
    disp8 = jnp.broadcast_to(disp_in[...], (8, disp_in.shape[1]))
    stiff = lax.dot_general(
        disp8, coupling[...], NT, precision=highest, preferred_element_type=jnp.float32
    )[0:1]
    vel_new = vel_in[...] + modal_step * (modal - stiff)
    vel_out[...] = vel_new
    disp_out[...] = disp_in[...] + modal_step * vel_new

    z_copy.wait_recv()
    column = z_in[...]
    for k in range(9):
        up, down = 3 * k + 2, 3 * k
        above = column if k == 0 else pltpu.roll(column, LANES - k, 1)
        cells[up] = jnp.where(
            lane == 0, jnp.where(at_bottom, inflow[up], above), pltpu.roll(cells[up], 1, 1)
        )
        cells[down] = jnp.where(
            lane == LANES - 1,
            jnp.where(at_bottom, pltpu.roll(column, LANES - 1 - k, 1), inflow[down]),
            pltpu.roll(cells[down], LANES - 1, 1),
        )

    ups = [i for i in range(27) if i // 3 % 3 == 2]
    downs = [i for i in range(27) if i // 3 % 3 == 0]
    for k in range(9):
        for x in range(size_x):
            spot = k * size_x + x
            last = (x + 1) * size_y - 1
            y_send[0, spot : spot + 1, :] = cells[ups[k], last : last + 1, :]
            first = x * size_y
            y_send[1, spot : spot + 1, :] = cells[downs[k], first : first + 1, :]
    y_copies = [
        send(y_send.at[0], y_in.at[0], (gx, lax.rem(gy + 1, columns), gz)),
        send(y_send.at[1], y_in.at[1], (gx, lax.rem(gy + columns - 1, columns), gz)),
    ]
    row = lax.broadcasted_iota(jnp.int32, (size_y, LANES), 0)
    for copy in y_copies:
        copy.wait_recv()
    for k in range(9):
        for x in range(size_x):
            spot = k * size_x + x
            span = slice(x * size_y, (x + 1) * size_y)
            up, down = ups[k], downs[k]
            below = jnp.where(gy == 0, inflow[up], y_in[0, spot : spot + 1, :])
            cells[up, span, :] = jnp.where(row == 0, below, pltpu.roll(cells[up, span, :], 1, 0))
            above = jnp.where(gy == columns - 1, inflow[down], y_in[1, spot : spot + 1, :])
            cells[down, span, :] = jnp.where(
                row == size_y - 1, above, pltpu.roll(cells[down, span, :], size_y - 1, 0)
            )

    tail = plane - size_y
    x_copies = [
        send(cells.at[pl.ds(18, 9), pl.ds(tail, size_y)], x_in.at[0], far_id(1)),
        send(cells.at[pl.ds(0, 9), pl.ds(0, size_y)], x_in.at[1], far_id(slabs - 1)),
    ]
    pops_out[9:18] = cells[9:18]
    pops_out[18:27, size_y:, :] = cells[18:27, :tail, :]
    pops_out[0:9, :tail, :] = cells[0:9, size_y:, :]
    for copy in x_copies:
        copy.wait_recv()
    pops_out[18:27, :size_y, :] = x_in[0]
    pops_out[0:9, tail:, :] = x_in[1]
    for copy in started:
        copy.wait_send()


def store_kernel(a, b, c, d, a_out, b_out, c_out, d_out, sems):
    pairs = [(a.at[pl.ds(i, 9)], a_out.at[pl.ds(i, 9)]) for i in (0, 9, 18)]
    pairs += [(b, b_out), (c, c_out), (d, d_out)]
    copies = [
        pltpu.make_async_copy(src, dst, sems.at[number])
        for number, (src, dst) in enumerate(pairs)
    ]
    for copy in copies:
        copy.start()
    for copy in copies:
        copy.wait()


def body(
    sizes,
    populations,
    relax,
    entry_point,
    entry_offset,
    entry_weight,
    entry_count,
    turbine_owner,
    mode_shapes,
    coupling,
    modal_disp,
    modal_vel,
    rigid_vel,
    drag_coef,
):
    slabs, columns, layers = sizes
    _, size_x, size_y, size_z = populations.shape
    points = drag_coef.shape[1]
    modes = modal_vel.shape[1]
    capacity = entry_point.shape[0]
    plane = size_x * size_y
    padded = -(-slabs // 8) * 8
    rows = 3 * padded
    ranks = columns * layers
    width = -(-3 * points // LANES) * LANES
    assert ranks == 8 and layers == 2 and size_z == LANES and points <= 8 * LANES
    copies = 2 * (slabs - 1) + 2 * (ranks - 1) + 5
    vmem = pl.BlockSpec(memory_space=pltpu.VMEM)
    hbm = pl.BlockSpec(memory_space=pltpu.HBM)
    whole = jnp.int32
    full = jnp.float32
    half = jnp.bfloat16
    out = pl.pallas_call(
        functools.partial(kernel, (slabs, columns, layers, points, size_x, size_y)),
        out_shape=(
            jax.ShapeDtypeStruct((27, plane, size_z), full),
            jax.ShapeDtypeStruct((3 * plane, size_z), full),
            jax.ShapeDtypeStruct((1, modes), full),
            jax.ShapeDtypeStruct((1, modes), full),
        ),
        in_specs=[hbm] * 13,
        out_specs=(vmem,) * 4,
        scratch_shapes=[
            pltpu.VMEM((27, plane, size_z), full),
            pltpu.SMEM(relax.shape, full),
            pltpu.VMEM((1, capacity), whole),
            pltpu.VMEM(entry_offset.shape, whole),
            pltpu.VMEM(entry_weight.shape, full),
            pltpu.SMEM(entry_count.shape, whole),
            pltpu.SMEM(turbine_owner.shape, whole),
            pltpu.VMEM((3 * points, modes), half),
            pltpu.VMEM((modes, modes), full),
            pltpu.VMEM((1, modes), full),
            pltpu.VMEM((1, modes), full),
            pltpu.VMEM((3, 1, points), full),
            pltpu.VMEM((1, points), full),
            pltpu.VMEM((8, 8 * LANES), full),
            pltpu.VMEM((27, plane, size_z), full),
            pltpu.VMEM((27, plane, size_z), full),
            pltpu.VMEM((3 * plane, 2 * LANES), half),
            pltpu.VMEM((TILE_SIDE, LANES, capacity), half),
            pltpu.VMEM((TILE_SIDE, plane, capacity), full),
            pltpu.VMEM((LANES, capacity), half),
            pltpu.VMEM((8, rows, LANES), full),
            pltpu.VMEM((ranks - 1, rows, LANES), full),
            pltpu.VMEM((rows, LANES), full),
            pltpu.VMEM((slabs - 1, rows, LANES), full),
            pltpu.VMEM((8, 8, LANES), full),
            pltpu.VMEM((slabs, 8, LANES), full),
            pltpu.VMEM((rows, LANES), full),
            pltpu.VMEM((8, rows, LANES), full),
            pltpu.VMEM((8, width), full),
            pltpu.VMEM((3 * plane, LANES), full),
            pltpu.VMEM((plane, LANES), full),
            pltpu.VMEM((plane, LANES), full),
            pltpu.VMEM((2, 9 * size_x + 4, LANES), full),
            pltpu.VMEM((2, 9 * size_x + 4, LANES), full),
            pltpu.VMEM((2, 9, size_y, LANES), full),
            pltpu.SemaphoreType.DMA((13,)),
            pltpu.SemaphoreType.DMA((copies,)),
            pltpu.SemaphoreType.DMA((copies,)),
        ],
        compiler_params=pltpu.CompilerParams(
            collective_id=0, has_side_effects=True, vmem_limit_bytes=VMEM_BYTES
        ),
    )(
        populations.reshape(27, plane, size_z),
        relax,
        entry_point[None, :],
        entry_offset,
        entry_weight,
        entry_count,
        turbine_owner,
        mode_shapes[0],
        coupling[0],
        modal_disp,
        modal_vel,
        rigid_vel.transpose(1, 0, 2),
        drag_coef,
    )
    populations_out, body_force, disp_new, vel_new = pl.pallas_call(
        store_kernel,
        out_shape=tuple(jax.ShapeDtypeStruct(o.shape, o.dtype) for o in out),
        in_specs=[hbm] * 4,
        out_specs=(hbm,) * 4,
        scratch_shapes=[pltpu.SemaphoreType.DMA((6,))],
        compiler_params=pltpu.CompilerParams(
            has_side_effects=True, vmem_limit_bytes=VMEM_BYTES
        ),
    )(*out)
    return (
        populations_out.reshape(populations.shape),
        body_force.reshape(3, size_x, size_y, size_z),
        disp_new,
        vel_new,
    )


def solution(mesh):
    sizes = (mesh.shape["gx"], mesh.shape["gy"], mesh.shape["gz"])
    return jax.shard_map(
        functools.partial(body, sizes),
        mesh=mesh,
        in_specs=(
            P(None, "gx", "gy", "gz"),
            P(),
            P(("gx", "gy", "gz")),
            P(None, ("gx", "gy", "gz")),
            P(None, ("gx", "gy", "gz")),
            P(("gx", "gy", "gz")),
            P(),
            P("gx", None, None),
            P("gx", None, None),
            P("gx", None),
            P("gx", None),
            P("gx", None, None),
            P("gx", None),
        ),
        out_specs=(
            P(None, "gx", "gy", "gz"),
            P(None, "gx", "gy", "gz"),
            P("gx", None),
            P("gx", None),
        ),
        check_vma=False,
    )
```

```python
import functools

import jax
import jax.numpy as jnp
import numpy as np
from jax import lax
from jax.experimental import pallas as pl
from jax.experimental.pallas import tpu as pltpu
from jax.sharding import PartitionSpec as P

TILE_SIDE = 4
LANES = 128
CHUNK = 256
VMEM_BYTES = 64 * 1024 * 1024
MESH = pl.DeviceIdType.MESH

highest = lax.Precision.HIGHEST
inflow_speed = 0.05
force_unit = 0.02
modal_step = 0.004

NT = (((1,), (1,)), ((), ()))
NN = (((1,), (0,)), ((), ()))


def inflow_values():
    steps = (-1.0, 0.0, 1.0)
    values = []
    for a in steps:
        for b in steps:
            for c in steps:
                weight = (8.0 / 27.0, 2.0 / 27.0, 1.0 / 54.0, 1.0 / 216.0)[
                    int(a * a + b * b + c * c)
                ]
                along = inflow_speed * a
                values.append(
                    weight
                    * (1.0 + 3.0 * along + 4.5 * along * along - 1.5 * inflow_speed * inflow_speed)
                )
    return [float(np.float32(v)) for v in values]


def transform(values, one):
    values = list(values)
    for stride in (9, 3, 1):
        for base in range(27):
            if base // stride % 3 == 0:
                spots = (base, base + stride, base + 2 * stride)
                for spot, value in zip(spots, one(*(values[s] for s in spots))):
                    values[spot] = value
    return values


def to_moments(low, mid, high):
    both = low + high
    return both + mid, high - low, both


def from_moments(zeroth, first, second):
    return 0.5 * (second - first), zeroth - second, 0.5 * (first + second)


def halves(value):
    high = value.astype(jnp.bfloat16)
    return high, (value - high.astype(jnp.float32)).astype(jnp.bfloat16)


def kernel(
    sizes,
    pops_hbm,
    relax_hbm,
    point_hbm,
    offset_hbm,
    weight_hbm,
    count_hbm,
    owner_hbm,
    shapes_hbm,
    coupling_hbm,
    disp_hbm,
    vel_hbm,
    rigid_hbm,
    drag_hbm,
    pops_hbm_out,
    force_hbm_out,
    disp_hbm_out,
    vel_hbm_out,
    force_out,
    disp_out,
    vel_out,
    pops,
    relax,
    point_in,
    offset_in,
    weight_in,
    count_in,
    owner_in,
    shapes,
    coupling,
    disp_in,
    vel_in,
    rigid_in,
    drag_in,
    aux_in,
    moments,
    cells,
    raw_pair,
    pick_z,
    kern_xy,
    pick_low,
    dense,
    dense_in,
    slab_sum,
    slab_in,
    aux,
    aux_all,
    blade,
    blade_all,
    erow,
    spread,
    z_send,
    z_in,
    y_send,
    y_in,
    x_in,
    copy_sem,
    store_sem,
    send_sem,
    recv_sem,
):
    slabs, columns, layers, points, size_x, size_y = sizes
    ranks = columns * layers
    padded = blade.shape[0] // 3
    rows = 3 * padded
    capacity = point_in.shape[1]
    plane = size_x * size_y
    gx = lax.axis_index("gx")
    gy = lax.axis_index("gy")
    gz = lax.axis_index("gz")
    rank = gy * layers + gz
    inflow = inflow_values()

    loads = {}
    for number, (name, src, dst) in enumerate(
        (
            ("pops", pops_hbm, pops),
            ("vel", vel_hbm, vel_in),
            ("rigid", rigid_hbm, rigid_in),
            ("drag", drag_hbm, drag_in),
            ("shapes", shapes_hbm, shapes),
            ("count", count_hbm, count_in),
            ("owner", owner_hbm, owner_in),
            ("point", point_hbm, point_in),
            ("offset", offset_hbm, offset_in),
            ("weight", weight_hbm, weight_in),
            ("relax", relax_hbm, relax),
            ("disp", disp_hbm, disp_in),
            ("coupling", coupling_hbm, coupling),
        )
    ):
        loads[name] = pltpu.make_async_copy(src, dst, copy_sem.at[number])
        loads[name].start()

    def slab_peer(step):
        return lax.rem(rank + step, ranks)

    def slab_id(other):
        return (gx, lax.div(other, layers), lax.rem(other, layers))

    def far_id(step):
        return (lax.rem(gx + step, slabs), gy, gz)

    barrier = pltpu.get_barrier_semaphore()
    for step in range(1, slabs):
        pl.semaphore_signal(barrier, inc=1, device_id=far_id(step), device_id_type=MESH)
    for step in range(1, ranks):
        pl.semaphore_signal(
            barrier, inc=1, device_id=slab_id(slab_peer(step)), device_id_type=MESH
        )

    stores = []

    def store(src, dst):
        copy = pltpu.make_async_copy(src, dst, store_sem.at[len(stores)])
        copy.start()
        stores.append(copy)

    used = [0]
    started = []

    def send(src, dst, device):
        copy = pltpu.make_async_remote_copy(
            src_ref=src,
            dst_ref=dst,
            send_sem=send_sem.at[used[0]],
            recv_sem=recv_sem.at[used[0]],
            device_id=device,
            device_id_type=MESH,
        )
        used[0] += 1
        copy.start()
        started.append(copy)
        return copy

    loads["pops"].wait()

    def moments_of(step, _):
        part = pl.ds(pl.multiple_of(step * 8, 8), 8)
        values = transform([pops[i, part, :] for i in range(27)], to_moments)
        for m in range(27):
            moments[m, part, :] = values[m]
        inverse = 1.0 / values[0]
        for c, m in enumerate((9, 3, 1)):
            raw = values[m] * inverse
            spot = pl.ds(pl.multiple_of(step * 8 + c * plane, 8), 8)
            spread[spot, :] = raw
        return 0

    lax.fori_loop(0, plane // 8, moments_of, 0)
    raw_high, raw_low = halves(spread[...])
    raw_pair[:, :LANES] = raw_high
    raw_pair[:, LANES:] = raw_low

    for name in ("vel", "rigid", "drag", "shapes"):
        loads[name].wait()
    aux_in[...] = jnp.zeros_like(aux_in)
    for d in range(3):
        aux_in[d : d + 1, :points] = rigid_in[d]
    aux_in[3:4, :points] = drag_in[...]
    vel8 = jnp.broadcast_to(vel_in[...], (8, vel_in.shape[1])).astype(jnp.bfloat16)
    erow[...] = jnp.zeros_like(erow)
    erow[:, : 3 * points] = lax.dot_general(
        vel8, shapes[...], NT, preferred_element_type=jnp.float32
    )
    width = erow.shape[1]
    line = erow[...]
    shifted = [
        line if c == 0 else pltpu.roll(line, width - c * points, 1) for c in range(3)
    ]
    row8 = lax.broadcasted_iota(jnp.int32, (8, LANES), 0)
    lane8 = lax.broadcasted_iota(jnp.int32, (8, LANES), 1)
    for jh in range(8):
        spot = slice(jh * LANES, (jh + 1) * LANES)
        both = jnp.where(
            row8 == 0,
            shifted[0][:, spot],
            jnp.where(row8 == 1, shifted[1][:, spot], shifted[2][:, spot]),
        )
        inside = (row8 < 3) & (lane8 + jh * LANES < points)
        aux[jh] = aux_in[:, spot] + jnp.where(inside, both, 0.0)
    pl.semaphore_wait(barrier, slabs - 1 + ranks - 1)
    aux_copies = [
        send(aux.at[rank], aux_all.at[gx], far_id(step)) for step in range(1, slabs)
    ]
    aux_all[gx] = aux[rank]

    for name in ("count", "owner", "point", "offset", "weight"):
        loads[name].wait()
    dense[...] = jnp.zeros_like(dense)
    count = count_in[0]
    iota_y = lax.broadcasted_iota(jnp.int32, (size_y, CHUNK), 0)
    iota_z = lax.broadcasted_iota(jnp.int32, (LANES, CHUNK), 0)
    iota_s = lax.broadcasted_iota(jnp.int32, (padded, CHUNK), 0)
    iota_r = lax.broadcasted_iota(jnp.int32, (1, CHUNK), 1)

    def slots_of(part):
        name = point_in[:, part]
        turbine = jnp.zeros_like(name)
        for t in range(1, slabs):
            turbine = turbine + jnp.where(name >= t * points, 1, 0)
        owner = jnp.zeros_like(name)
        for t in range(slabs):
            owner = owner + jnp.where(turbine == t, owner_in[t], 0)
        point = name - turbine * points
        high = lax.shift_right_logical(point, 7)
        masks = [(iota_s == owner) & (high == jh) for jh in range(8)]
        return point - high * LANES, masks

    def gather(step, _):
        base = pl.multiple_of(step * CHUNK, CHUNK)
        part = pl.ds(base, CHUNK)
        weight = jnp.where(iota_r + base < count, weight_in[:, part], 0.0)
        off_x = offset_in[0:1, part]
        off_y = offset_in[1:2, part]
        off_z = offset_in[2:3, part]
        at_y = [off_y + b == iota_y for b in range(TILE_SIDE)]
        by_x = []
        for x in range(size_x):
            value = jnp.zeros((16, CHUNK), jnp.float32)
            for a in range(TILE_SIDE):
                value = jnp.where(off_x + a == x, weight[16 * a : 16 * a + 16], value)
            by_x.append(value)
        total = [jnp.zeros((size_y, CHUNK), jnp.float32) for _ in range(3)]
        for c in range(TILE_SIDE):
            at_z = jnp.where(off_z + c == iota_z, 1.0, 0.0).astype(jnp.bfloat16)
            pick_z[c, :, part] = at_z
            layer = lax.dot_general(
                raw_pair[...],
                jnp.concatenate([at_z, at_z], axis=0),
                NN,
                preferred_element_type=jnp.float32,
            )
            for x in range(size_x):
                value = jnp.zeros((size_y, CHUNK), jnp.float32)
                for b in range(TILE_SIDE):
                    row = 4 * b + c
                    value = jnp.where(at_y[b], by_x[x][row : row + 1], value)
                kern_xy[c, x * size_y : (x + 1) * size_y, part] = value
                for d in range(3):
                    first = d * plane + x * size_y
                    total[d] = total[d] + value * layer[first : first + size_y]
        partial = [jnp.sum(t, axis=0, keepdims=True) for t in total]
        low, masks = slots_of(part)
        at_low = jnp.where(low == iota_z, 1.0, 0.0).astype(jnp.bfloat16)
        pick_low[:, part] = at_low
        placed = jnp.concatenate(
            [jnp.where(masks[jh], partial[d], 0.0) for jh in range(8) for d in range(3)], axis=0
        )
        high_part, low_part = halves(placed)
        dense[...] += (
            lax.dot_general(high_part, at_low, NT, preferred_element_type=jnp.float32)
            + lax.dot_general(low_part, at_low, NT, preferred_element_type=jnp.float32)
        ).reshape(8, rows, LANES)
        return 0

    lax.fori_loop(0, capacity // CHUNK, gather, 0)

    first_copies = [
        send(dense.at[slab_peer(step)], dense_in.at[step - 1], slab_id(slab_peer(step)))
        for step in range(1, ranks)
    ]
    own = dense[rank]
    for step in range(1, ranks):
        first_copies[step - 1].wait_recv()
        own = own + dense_in[step - 1]
    slab_sum[...] = own
    second_copies = [
        send(slab_sum, slab_in.at[step - 1], far_id(step)) for step in range(1, slabs)
    ]
    for copy in aux_copies:
        copy.wait_recv()
    for step in range(1, slabs):
        second_copies[step - 1].wait_recv()
        own = own + slab_in[step - 1]

    blade[...] = jnp.zeros_like(blade)
    for s in range(slabs):
        here = aux_all[s]
        relative = [
            own[d * padded + s : d * padded + s + 1] - here[d : d + 1] for d in range(3)
        ]
        speed = jnp.sqrt(
            relative[0] * relative[0] + relative[1] * relative[1] + relative[2] * relative[2]
        )
        factor = here[3:4] * speed
        for d in range(3):
            spot = d * padded + s
            blade[spot : spot + 1, :] = factor * relative[d]
    blade_all[rank] = blade[...]
    third_copies = [
        send(blade, blade_all.at[rank], slab_id(slab_peer(step))) for step in range(1, ranks)
    ]
    for copy in third_copies:
        copy.wait_recv()

    blade_high, blade_low = halves(blade_all[...].reshape(8 * rows, LANES))
    blade_pair = jnp.concatenate([blade_high, blade_low], axis=1)
    spread[...] = jnp.zeros_like(spread)

    def scatter(step, _):
        part = pl.ds(pl.multiple_of(step * CHUNK, CHUNK), CHUNK)
        _, masks = slots_of(part)
        at_low = pick_low[:, part]
        found = lax.dot_general(
            blade_pair,
            jnp.concatenate([at_low, at_low], axis=0),
            NN,
            preferred_element_type=jnp.float32,
        )
        forces = []
        for d in range(3):
            value = jnp.zeros((padded, CHUNK), jnp.float32)
            for jh in range(8):
                first = jh * rows + d * padded
                value = jnp.where(masks[jh], found[first : first + padded], value)
            forces.append(jnp.sum(value, axis=0, keepdims=True))
        total = jnp.zeros(spread.shape, jnp.float32)
        for c in range(TILE_SIDE):
            kern = kern_xy[c, :, part]
            high_part, low_part = halves(
                jnp.concatenate([kern * forces[d] for d in range(3)], axis=0)
            )
            at_z = pick_z[c, :, part]
            total = total + (
                lax.dot_general(high_part, at_z, NT, preferred_element_type=jnp.float32)
                + lax.dot_general(low_part, at_z, NT, preferred_element_type=jnp.float32)
            )
        spread[...] += total
        return 0

    lax.fori_loop(0, capacity // CHUNK, scatter, 0)
    force_out[...] = -spread[...]
    store(force_out, force_hbm_out)

    loads["relax"].wait()

    def collide(step, _):
        part = pl.ds(pl.multiple_of(step * 8, 8), 8)
        density = moments[0, part, :]
        inverse = 1.0 / density
        force = [
            force_unit * force_out[pl.ds(pl.multiple_of(step * 8 + d * plane, 8), 8), :]
            for d in range(3)
        ]
        velocity = [
            (moments[m, part, :] + 0.5 * force[d]) * inverse for d, m in enumerate((9, 3, 1))
        ]
        pushed = [density * v for v in velocity]
        pairs = {}
        sources = {}
        for d in range(3):
            for e in range(d, 3):
                pairs[d, e] = pushed[d] * velocity[e]
                sources[d, e] = velocity[d] * force[e] + velocity[e] * force[d]
        values = []
        for m in range(27):
            powers = (m // 9, m // 3 % 3, m % 3)
            odd = [d for d in range(3) if powers[d] == 1]
            even = [d for d in range(3) if powers[d] == 2]
            scale = (1.0 / 3.0) ** len(even)
            source = None
            if len(odd) == 0:
                wanted = density * scale
                if even:
                    square = pairs[even[0], even[0]]
                    source = sources[even[0], even[0]]
                    for d in even[1:]:
                        square = square + pairs[d, d]
                        source = source + sources[d, d]
                    wanted = wanted + square * (3.0 * scale)
                    source = source * (3.0 * scale)
            elif len(odd) == 1:
                wanted = pushed[odd[0]] * scale
                source = force[odd[0]] * scale
            elif len(odd) == 2:
                wanted = pairs[odd[0], odd[1]] * scale
                source = sources[odd[0], odd[1]] * scale
            else:
                wanted = None
            rate = relax[m]
            here = moments[m, part, :]
            gap = here if wanted is None else here - wanted
            value = -rate * gap
            if source is not None:
                value = value + (1.0 - 0.5 * rate) * source
            values.append(value)
        values = transform(values, from_moments)
        for i in range(27):
            cells[i, part, :] = pops[i, part, :] + values[i]
        return 0

    lax.fori_loop(0, plane // 8, collide, 0)

    lane = lax.broadcasted_iota(jnp.int32, (plane, LANES), 1)
    at_bottom = gz == 0
    packed = jnp.zeros((plane, LANES), jnp.float32)
    for k in range(9):
        column = jnp.where(
            at_bottom,
            pltpu.roll(cells[3 * k + 2], k + 1, 1),
            cells[3 * k] if k == 0 else pltpu.roll(cells[3 * k], k, 1),
        )
        packed = jnp.where(lane == k, column, packed)
    z_send[...] = packed
    z_copy = send(z_send, z_in, (gx, gy, 1 - gz))

    pieces = []
    for d in range(3):
        chunks = [
            jnp.broadcast_to(blade_all[jh, pl.ds(d * padded + gx, 1), :], (8, LANES))
            for jh in range(8)
        ]
        chunks.append(jnp.zeros((8, width - 8 * LANES), jnp.float32))
        piece = jnp.concatenate(chunks, axis=1)
        pieces.append(piece if d == 0 else pltpu.roll(piece, d * points, 1))
    erow[...] = pieces[0] + pieces[1] + pieces[2]
    modal = lax.dot_general(
        erow[:, : 3 * points].astype(jnp.bfloat16),
        shapes[...],
        NN,
        preferred_element_type=jnp.float32,
    )[0:1]
    loads["disp"].wait()
    loads["coupling"].wait()
    disp8 = jnp.broadcast_to(disp_in[...], (8, disp_in.shape[1]))
    stiff = lax.dot_general(
        disp8, coupling[...], NT, precision=highest, preferred_element_type=jnp.float32
    )[0:1]
    vel_new = vel_in[...] + modal_step * (modal - stiff)
    vel_out[...] = vel_new
    disp_out[...] = disp_in[...] + modal_step * vel_new
    store(vel_out, vel_hbm_out)
    store(disp_out, disp_hbm_out)

    z_copy.wait_recv()
    column = z_in[...]
    for k in range(9):
        up, down = 3 * k + 2, 3 * k
        above = column if k == 0 else pltpu.roll(column, LANES - k, 1)
        cells[up] = jnp.where(
            lane == 0, jnp.where(at_bottom, inflow[up], above), pltpu.roll(cells[up], 1, 1)
        )
        cells[down] = jnp.where(
            lane == LANES - 1,
            jnp.where(at_bottom, pltpu.roll(column, LANES - 1 - k, 1), inflow[down]),
            pltpu.roll(cells[down], LANES - 1, 1),
        )

    ups = [i for i in range(27) if i // 3 % 3 == 2]
    downs = [i for i in range(27) if i // 3 % 3 == 0]
    for k in range(9):
        for x in range(size_x):
            spot = k * size_x + x
            last = (x + 1) * size_y - 1
            y_send[0, spot : spot + 1, :] = cells[ups[k], last : last + 1, :]
            first = x * size_y
            y_send[1, spot : spot + 1, :] = cells[downs[k], first : first + 1, :]
    y_copies = [
        send(y_send.at[0], y_in.at[0], (gx, lax.rem(gy + 1, columns), gz)),
        send(y_send.at[1], y_in.at[1], (gx, lax.rem(gy + columns - 1, columns), gz)),
    ]
    row = lax.broadcasted_iota(jnp.int32, (size_y, LANES), 0)
    for copy in y_copies:
        copy.wait_recv()
    for k in range(9):
        for x in range(size_x):
            spot = k * size_x + x
            span = slice(x * size_y, (x + 1) * size_y)
            up, down = ups[k], downs[k]
            below = jnp.where(gy == 0, inflow[up], y_in[0, spot : spot + 1, :])
            cells[up, span, :] = jnp.where(row == 0, below, pltpu.roll(cells[up, span, :], 1, 0))
            above = jnp.where(gy == columns - 1, inflow[down], y_in[1, spot : spot + 1, :])
            cells[down, span, :] = jnp.where(
                row == size_y - 1, above, pltpu.roll(cells[down, span, :], size_y - 1, 0)
            )

    tail = plane - size_y
    x_copies = [
        send(cells.at[pl.ds(18, 9), pl.ds(tail, size_y)], x_in.at[0], far_id(1)),
        send(cells.at[pl.ds(0, 9), pl.ds(0, size_y)], x_in.at[1], far_id(slabs - 1)),
    ]
    low, mid, high = (pl.ds(i, 9) for i in (0, 9, 18))
    inner, outer = pl.ds(0, tail), pl.ds(size_y, tail)
    first, last = pl.ds(0, size_y), pl.ds(tail, size_y)
    store(cells.at[mid], pops_hbm_out.at[mid])
    store(cells.at[high, inner], pops_hbm_out.at[high, outer])
    store(cells.at[low, outer], pops_hbm_out.at[low, inner])
    x_copies[0].wait_recv()
    store(x_in.at[0], pops_hbm_out.at[high, first])
    x_copies[1].wait_recv()
    store(x_in.at[1], pops_hbm_out.at[low, last])
    for copy in stores:
        copy.wait()
    for copy in started:
        copy.wait_send()


def store_kernel(*refs):
    sources, targets, held = refs[0:4], refs[4:8], refs[8:12]
    load_sem, store_sem = refs[12:]
    parts = [(0, pl.ds(i, 9)) for i in (9, 18, 0)] + [(k, slice(None)) for k in (1, 2, 3)]
    loads, stores = [], []
    for number, (k, part) in enumerate(parts):
        here = held[k].at[part]
        loads.append(pltpu.make_async_copy(sources[k].at[part], here, load_sem.at[number]))
        stores.append(pltpu.make_async_copy(here, targets[k].at[part], store_sem.at[number]))
        loads[-1].start()
    for load, store in zip(loads, stores):
        load.wait()
        store.start()
    for store in stores:
        store.wait()


def body(
    sizes,
    populations,
    relax,
    entry_point,
    entry_offset,
    entry_weight,
    entry_count,
    turbine_owner,
    mode_shapes,
    coupling,
    modal_disp,
    modal_vel,
    rigid_vel,
    drag_coef,
):
    slabs, columns, layers = sizes
    _, size_x, size_y, size_z = populations.shape
    points = drag_coef.shape[1]
    modes = modal_vel.shape[1]
    capacity = entry_point.shape[0]
    plane = size_x * size_y
    padded = -(-slabs // 8) * 8
    rows = 3 * padded
    ranks = columns * layers
    width = -(-3 * points // LANES) * LANES
    assert ranks == 8 and layers == 2 and size_z == LANES and points <= 8 * LANES
    copies = 2 * (slabs - 1) + 2 * (ranks - 1) + 5
    hbm = pl.BlockSpec(memory_space=pltpu.HBM)
    whole = jnp.int32
    full = jnp.float32
    half = jnp.bfloat16
    out = pl.pallas_call(
        functools.partial(kernel, (slabs, columns, layers, points, size_x, size_y)),
        out_shape=(
            jax.ShapeDtypeStruct((27, plane, size_z), full),
            jax.ShapeDtypeStruct((3 * plane, size_z), full),
            jax.ShapeDtypeStruct((1, modes), full),
            jax.ShapeDtypeStruct((1, modes), full),
        ),
        in_specs=[hbm] * 13,
        out_specs=(hbm,) * 4,
        scratch_shapes=[
            pltpu.VMEM((3 * plane, size_z), full),
            pltpu.VMEM((1, modes), full),
            pltpu.VMEM((1, modes), full),
            pltpu.VMEM((27, plane, size_z), full),
            pltpu.SMEM(relax.shape, full),
            pltpu.VMEM((1, capacity), whole),
            pltpu.VMEM(entry_offset.shape, whole),
            pltpu.VMEM(entry_weight.shape, full),
            pltpu.SMEM(entry_count.shape, whole),
            pltpu.SMEM(turbine_owner.shape, whole),
            pltpu.VMEM((3 * points, modes), half),
            pltpu.VMEM((modes, modes), full),
            pltpu.VMEM((1, modes), full),
            pltpu.VMEM((1, modes), full),
            pltpu.VMEM((3, 1, points), full),
            pltpu.VMEM((1, points), full),
            pltpu.VMEM((8, 8 * LANES), full),
            pltpu.VMEM((27, plane, size_z), full),
            pltpu.VMEM((27, plane, size_z), full),
            pltpu.VMEM((3 * plane, 2 * LANES), half),
            pltpu.VMEM((TILE_SIDE, LANES, capacity), half),
            pltpu.VMEM((TILE_SIDE, plane, capacity), full),
            pltpu.VMEM((LANES, capacity), half),
            pltpu.VMEM((8, rows, LANES), full),
            pltpu.VMEM((ranks - 1, rows, LANES), full),
            pltpu.VMEM((rows, LANES), full),
            pltpu.VMEM((slabs - 1, rows, LANES), full),
            pltpu.VMEM((8, 8, LANES), full),
            pltpu.VMEM((slabs, 8, LANES), full),
            pltpu.VMEM((rows, LANES), full),
            pltpu.VMEM((8, rows, LANES), full),
            pltpu.VMEM((8, width), full),
            pltpu.VMEM((3 * plane, LANES), full),
            pltpu.VMEM((plane, LANES), full),
            pltpu.VMEM((plane, LANES), full),
            pltpu.VMEM((2, 9 * size_x + 4, LANES), full),
            pltpu.VMEM((2, 9 * size_x + 4, LANES), full),
            pltpu.VMEM((2, 9, size_y, LANES), full),
            pltpu.SemaphoreType.DMA((13,)),
            pltpu.SemaphoreType.DMA((8,)),
            pltpu.SemaphoreType.DMA((copies,)),
            pltpu.SemaphoreType.DMA((copies,)),
        ],
        compiler_params=pltpu.CompilerParams(
            collective_id=0, has_side_effects=True, vmem_limit_bytes=VMEM_BYTES
        ),
    )(
        populations.reshape(27, plane, size_z),
        relax,
        entry_point[None, :],
        entry_offset,
        entry_weight,
        entry_count,
        turbine_owner,
        mode_shapes[0],
        coupling[0],
        modal_disp,
        modal_vel,
        rigid_vel.transpose(1, 0, 2),
        drag_coef,
    )
    populations_out, body_force, disp_new, vel_new = pl.pallas_call(
        store_kernel,
        out_shape=tuple(jax.ShapeDtypeStruct(o.shape, o.dtype) for o in out),
        in_specs=[hbm] * 4,
        out_specs=(hbm,) * 4,
        scratch_shapes=[pltpu.VMEM(o.shape, o.dtype) for o in out]
        + [pltpu.SemaphoreType.DMA((6,))] * 2,
        compiler_params=pltpu.CompilerParams(
            has_side_effects=True, vmem_limit_bytes=VMEM_BYTES
        ),
    )(*out)
    return (
        populations_out.reshape(populations.shape),
        body_force.reshape(3, size_x, size_y, size_z),
        disp_new,
        vel_new,
    )


def solution(mesh):
    sizes = (mesh.shape["gx"], mesh.shape["gy"], mesh.shape["gz"])
    return jax.shard_map(
        functools.partial(body, sizes),
        mesh=mesh,
        in_specs=(
            P(None, "gx", "gy", "gz"),
            P(),
            P(("gx", "gy", "gz")),
            P(None, ("gx", "gy", "gz")),
            P(None, ("gx", "gy", "gz")),
            P(("gx", "gy", "gz")),
            P(),
            P("gx", None, None),
            P("gx", None, None),
            P("gx", None),
            P("gx", None),
            P("gx", None, None),
            P("gx", None),
        ),
        out_specs=(
            P(None, "gx", "gy", "gz"),
            P(None, "gx", "gy", "gz"),
            P("gx", None),
            P("gx", None),
        ),
        check_vma=False,
    )
```

```python
import functools

import jax
import jax.numpy as jnp
import numpy as np
from jax import lax
from jax.experimental import pallas as pl
from jax.experimental.pallas import tpu as pltpu
from jax.sharding import PartitionSpec as P

TILE_SIDE = 4
LANES = 128
CHUNK = 256
VMEM_BYTES = 64 * 1024 * 1024
MESH = pl.DeviceIdType.MESH

highest = lax.Precision.HIGHEST
inflow_speed = 0.05
force_unit = 0.02
modal_step = 0.004

NT = (((1,), (1,)), ((), ()))
NN = (((1,), (0,)), ((), ()))


def inflow_values():
    steps = (-1.0, 0.0, 1.0)
    values = []
    for a in steps:
        for b in steps:
            for c in steps:
                weight = (8.0 / 27.0, 2.0 / 27.0, 1.0 / 54.0, 1.0 / 216.0)[
                    int(a * a + b * b + c * c)
                ]
                along = inflow_speed * a
                values.append(
                    weight
                    * (1.0 + 3.0 * along + 4.5 * along * along - 1.5 * inflow_speed * inflow_speed)
                )
    return [float(np.float32(v)) for v in values]


def transform(values, one):
    values = list(values)
    for stride in (9, 3, 1):
        for base in range(27):
            if base // stride % 3 == 0:
                spots = (base, base + stride, base + 2 * stride)
                for spot, value in zip(spots, one(*(values[s] for s in spots))):
                    values[spot] = value
    return values


def to_moments(low, mid, high):
    both = low + high
    return both + mid, high - low, both


def from_moments(zeroth, first, second):
    return 0.5 * (second - first), zeroth - second, 0.5 * (first + second)


def halves(value):
    high = value.astype(jnp.bfloat16)
    return high, (value - high.astype(jnp.float32)).astype(jnp.bfloat16)


def kernel(
    sizes,
    pops_hbm,
    relax_hbm,
    point_hbm,
    offset_hbm,
    weight_hbm,
    count_hbm,
    owner_hbm,
    shapes_hbm,
    coupling_hbm,
    disp_hbm,
    vel_hbm,
    rigid_hbm,
    drag_hbm,
    pops_hbm_out,
    force_hbm_out,
    disp_hbm_out,
    vel_hbm_out,
    force_out,
    disp_out,
    vel_out,
    pops,
    relax,
    point_in,
    offset_in,
    weight_in,
    count_in,
    owner_in,
    shapes,
    coupling,
    disp_in,
    vel_in,
    rigid_in,
    drag_in,
    aux_in,
    moments,
    cells,
    raw_pair,
    pick_z,
    kern_xy,
    pick_low,
    dense,
    dense_in,
    slab_sum,
    slab_in,
    aux,
    aux_all,
    blade,
    blade_all,
    erow,
    spread,
    z_send,
    z_in,
    y_send,
    y_in,
    z_edge,
    x_in,
    copy_sem,
    store_sem,
    send_sem,
    recv_sem,
):
    slabs, columns, layers, points, size_x, size_y = sizes
    ranks = columns * layers
    padded = blade.shape[0] // 3
    rows = 3 * padded
    capacity = point_in.shape[1]
    plane = size_x * size_y
    gx = lax.axis_index("gx")
    gy = lax.axis_index("gy")
    gz = lax.axis_index("gz")
    rank = gy * layers + gz
    inflow = inflow_values()

    loads = {}
    for number, (name, src, dst) in enumerate(
        (
            ("pops", pops_hbm, pops),
            ("count", count_hbm, count_in),
            ("owner", owner_hbm, owner_in),
            ("point", point_hbm, point_in),
            ("offset", offset_hbm, offset_in),
            ("weight", weight_hbm, weight_in),
            ("vel", vel_hbm, vel_in),
            ("rigid", rigid_hbm, rigid_in),
            ("drag", drag_hbm, drag_in),
            ("shapes", shapes_hbm, shapes),
            ("relax", relax_hbm, relax),
            ("disp", disp_hbm, disp_in),
            ("coupling", coupling_hbm, coupling),
        )
    ):
        loads[name] = pltpu.make_async_copy(src, dst, copy_sem.at[number])
        loads[name].start()

    def slab_peer(step):
        return lax.rem(rank + step, ranks)

    def slab_id(other):
        return (gx, lax.div(other, layers), lax.rem(other, layers))

    def far_id(step):
        return (lax.rem(gx + step, slabs), gy, gz)

    barrier = pltpu.get_barrier_semaphore()
    for step in range(1, slabs):
        pl.semaphore_signal(barrier, inc=1, device_id=far_id(step), device_id_type=MESH)
    for step in range(1, ranks):
        pl.semaphore_signal(
            barrier, inc=1, device_id=slab_id(slab_peer(step)), device_id_type=MESH
        )

    stores = []

    def store(src, dst):
        copy = pltpu.make_async_copy(src, dst, store_sem.at[len(stores)])
        copy.start()
        stores.append(copy)

    used = [0]
    started = []

    def send(src, dst, device):
        copy = pltpu.make_async_remote_copy(
            src_ref=src,
            dst_ref=dst,
            send_sem=send_sem.at[used[0]],
            recv_sem=recv_sem.at[used[0]],
            device_id=device,
            device_id_type=MESH,
        )
        used[0] += 1
        copy.start()
        started.append(copy)
        return copy

    loads["pops"].wait()

    def moments_of(step, _):
        part = pl.ds(pl.multiple_of(step * 8, 8), 8)
        values = transform([pops[i, part, :] for i in range(27)], to_moments)
        for m in range(27):
            moments[m, part, :] = values[m]
        inverse = 1.0 / values[0]
        for c, m in enumerate((9, 3, 1)):
            raw = values[m] * inverse
            spot = pl.ds(pl.multiple_of(step * 8 + c * plane, 8), 8)
            spread[spot, :] = raw
        return 0

    lax.fori_loop(0, plane // 8, moments_of, 0)
    raw_high, raw_low = halves(spread[...])
    raw_pair[:, :LANES] = raw_high
    raw_pair[:, LANES:] = raw_low

    for name in ("count", "owner", "point", "offset", "weight"):
        loads[name].wait()
    dense[...] = jnp.zeros_like(dense)
    count = count_in[0]
    iota_y = lax.broadcasted_iota(jnp.int32, (size_y, CHUNK), 0)
    iota_z = lax.broadcasted_iota(jnp.int32, (LANES, CHUNK), 0)
    iota_s = lax.broadcasted_iota(jnp.int32, (padded, CHUNK), 0)
    iota_r = lax.broadcasted_iota(jnp.int32, (1, CHUNK), 1)

    def slots_of(part):
        name = point_in[:, part]
        turbine = jnp.zeros_like(name)
        for t in range(1, slabs):
            turbine = turbine + jnp.where(name >= t * points, 1, 0)
        owner = jnp.zeros_like(name)
        for t in range(slabs):
            owner = owner + jnp.where(turbine == t, owner_in[t], 0)
        point = name - turbine * points
        high = lax.shift_right_logical(point, 7)
        masks = [(iota_s == owner) & (high == jh) for jh in range(8)]
        return point - high * LANES, masks

    def gather(step, _):
        base = pl.multiple_of(step * CHUNK, CHUNK)
        part = pl.ds(base, CHUNK)
        weight = jnp.where(iota_r + base < count, weight_in[:, part], 0.0)
        off_x = offset_in[0:1, part]
        off_y = offset_in[1:2, part]
        off_z = offset_in[2:3, part]
        at_y = [off_y + b == iota_y for b in range(TILE_SIDE)]
        by_x = []
        for x in range(size_x):
            value = jnp.zeros((16, CHUNK), jnp.float32)
            for a in range(TILE_SIDE):
                value = jnp.where(off_x + a == x, weight[16 * a : 16 * a + 16], value)
            by_x.append(value)
        total = [jnp.zeros((size_y, CHUNK), jnp.float32) for _ in range(3)]
        for c in range(TILE_SIDE):
            at_z = jnp.where(off_z + c == iota_z, 1.0, 0.0).astype(jnp.bfloat16)
            pick_z[c, :, part] = at_z
            layer = lax.dot_general(
                raw_pair[...],
                jnp.concatenate([at_z, at_z], axis=0),
                NN,
                preferred_element_type=jnp.float32,
            )
            for x in range(size_x):
                value = jnp.zeros((size_y, CHUNK), jnp.float32)
                for b in range(TILE_SIDE):
                    row = 4 * b + c
                    value = jnp.where(at_y[b], by_x[x][row : row + 1], value)
                kern_xy[c, x * size_y : (x + 1) * size_y, part] = value
                for d in range(3):
                    first = d * plane + x * size_y
                    total[d] = total[d] + value * layer[first : first + size_y]
        partial = [jnp.sum(t, axis=0, keepdims=True) for t in total]
        low, masks = slots_of(part)
        at_low = jnp.where(low == iota_z, 1.0, 0.0).astype(jnp.bfloat16)
        pick_low[:, part] = at_low
        placed = jnp.concatenate(
            [jnp.where(masks[jh], partial[d], 0.0) for jh in range(8) for d in range(3)], axis=0
        )
        high_part, low_part = halves(placed)
        dense[...] += (
            lax.dot_general(high_part, at_low, NT, preferred_element_type=jnp.float32)
            + lax.dot_general(low_part, at_low, NT, preferred_element_type=jnp.float32)
        ).reshape(8, rows, LANES)
        return 0

    lax.fori_loop(0, capacity // CHUNK, gather, 0)

    pl.semaphore_wait(barrier, slabs - 1 + ranks - 1)

    first_copies = [
        send(dense.at[slab_peer(step)], dense_in.at[step - 1], slab_id(slab_peer(step)))
        for step in range(1, ranks)
    ]
    for name in ("vel", "rigid", "drag", "shapes"):
        loads[name].wait()
    aux_in[...] = jnp.zeros_like(aux_in)
    for d in range(3):
        aux_in[d : d + 1, :points] = rigid_in[d]
    aux_in[3:4, :points] = drag_in[...]
    vel8 = jnp.broadcast_to(vel_in[...], (8, vel_in.shape[1])).astype(jnp.bfloat16)
    erow[...] = jnp.zeros_like(erow)
    erow[:, : 3 * points] = lax.dot_general(
        vel8, shapes[...], NT, preferred_element_type=jnp.float32
    )
    width = erow.shape[1]
    line = erow[...]
    shifted = [
        line if c == 0 else pltpu.roll(line, width - c * points, 1) for c in range(3)
    ]
    row8 = lax.broadcasted_iota(jnp.int32, (8, LANES), 0)
    lane8 = lax.broadcasted_iota(jnp.int32, (8, LANES), 1)
    for jh in range(8):
        spot = slice(jh * LANES, (jh + 1) * LANES)
        both = jnp.where(
            row8 == 0,
            shifted[0][:, spot],
            jnp.where(row8 == 1, shifted[1][:, spot], shifted[2][:, spot]),
        )
        inside = (row8 < 3) & (lane8 + jh * LANES < points)
        aux[jh] = aux_in[:, spot] + jnp.where(inside, both, 0.0)
    aux_copies = [
        send(aux.at[rank], aux_all.at[gx], far_id(step)) for step in range(1, slabs)
    ]
    aux_all[gx] = aux[rank]

    own = dense[rank]
    for step in range(1, ranks):
        first_copies[step - 1].wait_recv()
        own = own + dense_in[step - 1]
    slab_sum[...] = own
    second_copies = [
        send(slab_sum, slab_in.at[step - 1], far_id(step)) for step in range(1, slabs)
    ]
    for copy in aux_copies:
        copy.wait_recv()
    for step in range(1, slabs):
        second_copies[step - 1].wait_recv()
        own = own + slab_in[step - 1]

    blade[...] = jnp.zeros_like(blade)
    for s in range(slabs):
        here = aux_all[s]
        relative = [
            own[d * padded + s : d * padded + s + 1] - here[d : d + 1] for d in range(3)
        ]
        speed = jnp.sqrt(
            relative[0] * relative[0] + relative[1] * relative[1] + relative[2] * relative[2]
        )
        factor = here[3:4] * speed
        for d in range(3):
            spot = d * padded + s
            blade[spot : spot + 1, :] = factor * relative[d]
    blade_all[rank] = blade[...]
    third_copies = [
        send(blade, blade_all.at[rank], slab_id(slab_peer(step))) for step in range(1, ranks)
    ]
    for copy in third_copies:
        copy.wait_recv()

    blade_high, blade_low = halves(blade_all[...].reshape(8 * rows, LANES))
    blade_pair = jnp.concatenate([blade_high, blade_low], axis=1)
    spread[...] = jnp.zeros_like(spread)

    def scatter(step, _):
        part = pl.ds(pl.multiple_of(step * CHUNK, CHUNK), CHUNK)
        _, masks = slots_of(part)
        at_low = pick_low[:, part]
        found = lax.dot_general(
            blade_pair,
            jnp.concatenate([at_low, at_low], axis=0),
            NN,
            preferred_element_type=jnp.float32,
        )
        forces = []
        for d in range(3):
            value = jnp.zeros((padded, CHUNK), jnp.float32)
            for jh in range(8):
                first = jh * rows + d * padded
                value = jnp.where(masks[jh], found[first : first + padded], value)
            forces.append(jnp.sum(value, axis=0, keepdims=True))
        total = jnp.zeros(spread.shape, jnp.float32)
        for c in range(TILE_SIDE):
            kern = kern_xy[c, :, part]
            weighted = jnp.concatenate(
                [(kern * forces[d]).astype(jnp.bfloat16) for d in range(3)], axis=0
            )
            total = total + lax.dot_general(
                weighted, pick_z[c, :, part], NT, preferred_element_type=jnp.float32
            )
        spread[...] += total
        return 0

    lax.fori_loop(0, capacity // CHUNK, scatter, 0)
    force_out[...] = -spread[...]
    store(force_out, force_hbm_out)

    loads["relax"].wait()

    def collide(step, _):
        part = pl.ds(pl.multiple_of(step * 8, 8), 8)
        density = moments[0, part, :]
        inverse = 1.0 / density
        force = [
            force_unit * force_out[pl.ds(pl.multiple_of(step * 8 + d * plane, 8), 8), :]
            for d in range(3)
        ]
        velocity = [
            (moments[m, part, :] + 0.5 * force[d]) * inverse for d, m in enumerate((9, 3, 1))
        ]
        pushed = [density * v for v in velocity]
        pairs = {}
        sources = {}
        for d in range(3):
            for e in range(d, 3):
                pairs[d, e] = pushed[d] * velocity[e]
                sources[d, e] = velocity[d] * force[e] + velocity[e] * force[d]
        values = []
        for m in range(27):
            powers = (m // 9, m // 3 % 3, m % 3)
            odd = [d for d in range(3) if powers[d] == 1]
            even = [d for d in range(3) if powers[d] == 2]
            scale = (1.0 / 3.0) ** len(even)
            source = None
            if len(odd) == 0:
                wanted = density * scale
                if even:
                    square = pairs[even[0], even[0]]
                    source = sources[even[0], even[0]]
                    for d in even[1:]:
                        square = square + pairs[d, d]
                        source = source + sources[d, d]
                    wanted = wanted + square * (3.0 * scale)
                    source = source * (3.0 * scale)
            elif len(odd) == 1:
                wanted = pushed[odd[0]] * scale
                source = force[odd[0]] * scale
            elif len(odd) == 2:
                wanted = pairs[odd[0], odd[1]] * scale
                source = sources[odd[0], odd[1]] * scale
            else:
                wanted = None
            rate = relax[m]
            here = moments[m, part, :]
            gap = here if wanted is None else here - wanted
            value = -rate * gap
            if source is not None:
                value = value + (1.0 - 0.5 * rate) * source
            values.append(value)
        values = transform(values, from_moments)
        for i in range(27):
            cells[i, part, :] = pops[i, part, :] + values[i]
        return 0

    lax.fori_loop(0, plane // 8, collide, 0)

    lane = lax.broadcasted_iota(jnp.int32, (plane, LANES), 1)
    at_bottom = gz == 0
    packed = jnp.zeros((plane, LANES), jnp.float32)
    for k in range(9):
        column = jnp.where(
            at_bottom,
            pltpu.roll(cells[3 * k + 2], k + 1, 1),
            cells[3 * k] if k == 0 else pltpu.roll(cells[3 * k], k, 1),
        )
        packed = jnp.where(lane == k, column, packed)
    z_send[...] = packed
    next_y = lax.rem(gy + 1, columns)
    past_y = lax.rem(gy + columns - 1, columns)
    edge_copies = [
        send(z_send, z_in.at[0], (gx, gy, 1 - gz)),
        send(z_send, z_in.at[1], (gx, next_y, 1 - gz)),
        send(z_send, z_in.at[2], (gx, past_y, 1 - gz)),
    ]
    ups = [i for i in range(27) if i // 3 % 3 == 2]
    downs = [i for i in range(27) if i // 3 % 3 == 0]
    for k in range(9):
        for x in range(size_x):
            last = (x + 1) * size_y - 1
            y_send[0, k, x : x + 1, :] = cells[ups[k], last : last + 1, :]
            first = x * size_y
            y_send[1, k, x : x + 1, :] = cells[downs[k], first : first + 1, :]
    edge_copies += [
        send(y_send.at[0], y_in.at[0], (gx, next_y, gz)),
        send(y_send.at[1], y_in.at[1], (gx, past_y, gz)),
    ]
    for k in range(9):
        cells[3 * k + 2] = pltpu.roll(cells[3 * k + 2], 1, 1)
        cells[3 * k] = pltpu.roll(cells[3 * k], LANES - 1, 1)

    pieces = []
    for d in range(3):
        chunks = [
            jnp.broadcast_to(blade_all[jh, pl.ds(d * padded + gx, 1), :], (8, LANES))
            for jh in range(8)
        ]
        chunks.append(jnp.zeros((8, width - 8 * LANES), jnp.float32))
        piece = jnp.concatenate(chunks, axis=1)
        pieces.append(piece if d == 0 else pltpu.roll(piece, d * points, 1))
    erow[...] = pieces[0] + pieces[1] + pieces[2]
    modal = lax.dot_general(
        erow[:, : 3 * points].astype(jnp.bfloat16),
        shapes[...],
        NN,
        preferred_element_type=jnp.float32,
    )[0:1]
    loads["disp"].wait()
    loads["coupling"].wait()
    disp8 = jnp.broadcast_to(disp_in[...], (8, disp_in.shape[1]))
    stiff = lax.dot_general(
        disp8, coupling[...], NT, precision=highest, preferred_element_type=jnp.float32
    )[0:1]
    vel_new = vel_in[...] + modal_step * (modal - stiff)
    vel_out[...] = vel_new
    disp_out[...] = disp_in[...] + modal_step * vel_new
    store(vel_out, vel_hbm_out)
    store(disp_out, disp_hbm_out)

    def fill_lanes(k, side, column, rolled, lanes):
        if side == 2:
            above = column if k == 0 else pltpu.roll(column, LANES - k, 1)
            return jnp.where(
                lanes == 0, jnp.where(at_bottom, inflow[3 * k + 2], above), rolled
            )
        below = pltpu.roll(column, LANES - 1 - k, 1)
        return jnp.where(
            lanes == LANES - 1, jnp.where(at_bottom, below, inflow[3 * k]), rolled
        )

    for copy in edge_copies:
        copy.wait_recv()
    column = z_in[0]
    for k in range(9):
        for side in (0, 2):
            i = 3 * k + side
            cells[i] = fill_lanes(k, side, column, cells[i], lane)

    row = lax.broadcasted_iota(jnp.int32, (size_y, LANES), 0)
    z_edge[...] = jnp.zeros_like(z_edge)
    for x in range(size_x):
        last = (x + 1) * size_y - 1
        z_edge[0, x : x + 1, :] = z_in[1, last : last + 1, :]
        z_edge[1, x : x + 1, :] = z_in[2, x * size_y : x * size_y + 1, :]
    at_front, at_back = gy == 0, gy == columns - 1
    for k in range(9):
        for way, i in ((0, ups[k]), (1, downs[k])):
            halo = y_in[way, k]
            side = i % 3
            if side == 2:
                halo = fill_lanes(i // 3, 2, z_edge[way], pltpu.roll(halo, 1, 1), lane8)
            elif side == 0:
                halo = fill_lanes(i // 3, 0, z_edge[way], pltpu.roll(halo, LANES - 1, 1), lane8)
            halo = jnp.where(at_back if way else at_front, inflow[i], halo)
            for x in range(size_x):
                span = slice(x * size_y, (x + 1) * size_y)
                moved = pltpu.roll(cells[i, span, :], size_y - 1 if way else 1, 0)
                edge = size_y - 1 if way else 0
                cells[i, span, :] = jnp.where(row == edge, halo[x : x + 1], moved)

    tail = plane - size_y
    x_copies = [
        send(cells.at[pl.ds(18, 9), pl.ds(tail, size_y)], x_in.at[0], far_id(1)),
        send(cells.at[pl.ds(0, 9), pl.ds(0, size_y)], x_in.at[1], far_id(slabs - 1)),
    ]
    low, mid, high = (pl.ds(i, 9) for i in (0, 9, 18))
    inner, outer = pl.ds(0, tail), pl.ds(size_y, tail)
    first, last = pl.ds(0, size_y), pl.ds(tail, size_y)
    store(cells.at[mid], pops_hbm_out.at[mid])
    store(cells.at[high, inner], pops_hbm_out.at[high, outer])
    store(cells.at[low, outer], pops_hbm_out.at[low, inner])
    x_copies[0].wait_recv()
    store(x_in.at[0], pops_hbm_out.at[high, first])
    x_copies[1].wait_recv()
    store(x_in.at[1], pops_hbm_out.at[low, last])
    for copy in stores:
        copy.wait()
    for copy in started:
        copy.wait_send()


def store_kernel(*refs):
    sources, targets, held = refs[0:4], refs[4:8], refs[8:12]
    load_sem, store_sem = refs[12:]
    parts = [(0, pl.ds(i, 9)) for i in (9, 18, 0)] + [(k, slice(None)) for k in (1, 2, 3)]
    loads, stores = [], []
    for number, (k, part) in enumerate(parts):
        here = held[k].at[part]
        loads.append(pltpu.make_async_copy(sources[k].at[part], here, load_sem.at[number]))
        stores.append(pltpu.make_async_copy(here, targets[k].at[part], store_sem.at[number]))
        loads[-1].start()
    for load, store in zip(loads, stores):
        load.wait()
        store.start()
    for store in stores:
        store.wait()


def body(
    sizes,
    populations,
    relax,
    entry_point,
    entry_offset,
    entry_weight,
    entry_count,
    turbine_owner,
    mode_shapes,
    coupling,
    modal_disp,
    modal_vel,
    rigid_vel,
    drag_coef,
):
    slabs, columns, layers = sizes
    _, size_x, size_y, size_z = populations.shape
    points = drag_coef.shape[1]
    modes = modal_vel.shape[1]
    capacity = entry_point.shape[0]
    plane = size_x * size_y
    padded = -(-slabs // 8) * 8
    rows = 3 * padded
    ranks = columns * layers
    width = -(-3 * points // LANES) * LANES
    assert ranks == 8 and layers == 2 and size_z == LANES and points <= 8 * LANES
    assert columns > 2 and size_x <= 8
    copies = 2 * (slabs - 1) + 2 * (ranks - 1) + 7
    hbm = pl.BlockSpec(memory_space=pltpu.HBM)
    whole = jnp.int32
    full = jnp.float32
    half = jnp.bfloat16
    out = pl.pallas_call(
        functools.partial(kernel, (slabs, columns, layers, points, size_x, size_y)),
        out_shape=(
            jax.ShapeDtypeStruct((27, plane, size_z), full),
            jax.ShapeDtypeStruct((3 * plane, size_z), full),
            jax.ShapeDtypeStruct((1, modes), full),
            jax.ShapeDtypeStruct((1, modes), full),
        ),
        in_specs=[hbm] * 13,
        out_specs=(hbm,) * 4,
        scratch_shapes=[
            pltpu.VMEM((3 * plane, size_z), full),
            pltpu.VMEM((1, modes), full),
            pltpu.VMEM((1, modes), full),
            pltpu.VMEM((27, plane, size_z), full),
            pltpu.SMEM(relax.shape, full),
            pltpu.VMEM((1, capacity), whole),
            pltpu.VMEM(entry_offset.shape, whole),
            pltpu.VMEM(entry_weight.shape, full),
            pltpu.SMEM(entry_count.shape, whole),
            pltpu.SMEM(turbine_owner.shape, whole),
            pltpu.VMEM((3 * points, modes), half),
            pltpu.VMEM((modes, modes), full),
            pltpu.VMEM((1, modes), full),
            pltpu.VMEM((1, modes), full),
            pltpu.VMEM((3, 1, points), full),
            pltpu.VMEM((1, points), full),
            pltpu.VMEM((8, 8 * LANES), full),
            pltpu.VMEM((27, plane, size_z), full),
            pltpu.VMEM((27, plane, size_z), full),
            pltpu.VMEM((3 * plane, 2 * LANES), half),
            pltpu.VMEM((TILE_SIDE, LANES, capacity), half),
            pltpu.VMEM((TILE_SIDE, plane, capacity), full),
            pltpu.VMEM((LANES, capacity), half),
            pltpu.VMEM((8, rows, LANES), full),
            pltpu.VMEM((ranks - 1, rows, LANES), full),
            pltpu.VMEM((rows, LANES), full),
            pltpu.VMEM((slabs - 1, rows, LANES), full),
            pltpu.VMEM((8, 8, LANES), full),
            pltpu.VMEM((slabs, 8, LANES), full),
            pltpu.VMEM((rows, LANES), full),
            pltpu.VMEM((8, rows, LANES), full),
            pltpu.VMEM((8, width), full),
            pltpu.VMEM((3 * plane, LANES), full),
            pltpu.VMEM((plane, LANES), full),
            pltpu.VMEM((3, plane, LANES), full),
            pltpu.VMEM((2, 9, 8, LANES), full),
            pltpu.VMEM((2, 9, 8, LANES), full),
            pltpu.VMEM((2, 8, LANES), full),
            pltpu.VMEM((2, 9, size_y, LANES), full),
            pltpu.SemaphoreType.DMA((13,)),
            pltpu.SemaphoreType.DMA((8,)),
            pltpu.SemaphoreType.DMA((copies,)),
            pltpu.SemaphoreType.DMA((copies,)),
        ],
        compiler_params=pltpu.CompilerParams(
            collective_id=0, has_side_effects=True, vmem_limit_bytes=VMEM_BYTES
        ),
    )(
        populations.reshape(27, plane, size_z),
        relax,
        entry_point[None, :],
        entry_offset,
        entry_weight,
        entry_count,
        turbine_owner,
        mode_shapes[0],
        coupling[0],
        modal_disp,
        modal_vel,
        rigid_vel.transpose(1, 0, 2),
        drag_coef,
    )
    populations_out, body_force, disp_new, vel_new = pl.pallas_call(
        store_kernel,
        out_shape=tuple(jax.ShapeDtypeStruct(o.shape, o.dtype) for o in out),
        in_specs=[hbm] * 4,
        out_specs=(hbm,) * 4,
        scratch_shapes=[pltpu.VMEM(o.shape, o.dtype) for o in out]
        + [pltpu.SemaphoreType.DMA((6,))] * 2,
        compiler_params=pltpu.CompilerParams(
            has_side_effects=True, vmem_limit_bytes=VMEM_BYTES
        ),
    )(*out)
    return (
        populations_out.reshape(populations.shape),
        body_force.reshape(3, size_x, size_y, size_z),
        disp_new,
        vel_new,
    )


def solution(mesh):
    sizes = (mesh.shape["gx"], mesh.shape["gy"], mesh.shape["gz"])
    return jax.shard_map(
        functools.partial(body, sizes),
        mesh=mesh,
        in_specs=(
            P(None, "gx", "gy", "gz"),
            P(),
            P(("gx", "gy", "gz")),
            P(None, ("gx", "gy", "gz")),
            P(None, ("gx", "gy", "gz")),
            P(("gx", "gy", "gz")),
            P(),
            P("gx", None, None),
            P("gx", None, None),
            P("gx", None),
            P("gx", None),
            P("gx", None, None),
            P("gx", None),
        ),
        out_specs=(
            P(None, "gx", "gy", "gz"),
            P(None, "gx", "gy", "gz"),
            P("gx", None),
            P("gx", None),
        ),
        check_vma=False,
    )
```

```python
import functools

import jax
import jax.numpy as jnp
import numpy as np
from jax import lax
from jax.experimental import pallas as pl
from jax.experimental.pallas import tpu as pltpu
from jax.sharding import PartitionSpec as P

TILE_SIDE = 4
LANES = 128
CHUNK = 256
VMEM_BYTES = 64 * 1024 * 1024
MESH = pl.DeviceIdType.MESH

highest = lax.Precision.HIGHEST
inflow_speed = 0.05
force_unit = 0.02
modal_step = 0.004

NT = (((1,), (1,)), ((), ()))
NN = (((1,), (0,)), ((), ()))


def inflow_values():
    steps = (-1.0, 0.0, 1.0)
    values = []
    for a in steps:
        for b in steps:
            for c in steps:
                weight = (8.0 / 27.0, 2.0 / 27.0, 1.0 / 54.0, 1.0 / 216.0)[
                    int(a * a + b * b + c * c)
                ]
                along = inflow_speed * a
                values.append(
                    weight
                    * (1.0 + 3.0 * along + 4.5 * along * along - 1.5 * inflow_speed * inflow_speed)
                )
    return [float(np.float32(v)) for v in values]


def transform(values, one):
    values = list(values)
    for stride in (9, 3, 1):
        for base in range(27):
            if base // stride % 3 == 0:
                spots = (base, base + stride, base + 2 * stride)
                for spot, value in zip(spots, one(*(values[s] for s in spots))):
                    values[spot] = value
    return values


def to_moments(low, mid, high):
    both = low + high
    return both + mid, high - low, both


def from_moments(zeroth, first, second):
    return 0.5 * (second - first), zeroth - second, 0.5 * (first + second)


def halves(value):
    high = value.astype(jnp.bfloat16)
    return high, (value - high.astype(jnp.float32)).astype(jnp.bfloat16)


def kernel(
    sizes,
    pops_hbm,
    relax_hbm,
    point_hbm,
    offset_hbm,
    weight_hbm,
    count_hbm,
    owner_hbm,
    shapes_hbm,
    coupling_hbm,
    disp_hbm,
    vel_hbm,
    rigid_hbm,
    drag_hbm,
    pops_hbm_out,
    force_hbm_out,
    disp_hbm_out,
    vel_hbm_out,
    force_out,
    disp_out,
    vel_out,
    pops,
    relax,
    point_in,
    offset_in,
    weight_in,
    count_in,
    owner_in,
    shapes,
    coupling,
    disp_in,
    vel_in,
    rigid_in,
    drag_in,
    aux_in,
    moments,
    cells,
    raw_pair,
    pick_z,
    kern_xy,
    pick_low,
    dense,
    dense_in,
    slab_sum,
    slab_in,
    aux,
    aux_all,
    blade,
    blade_all,
    erow,
    spread,
    z_send,
    z_in,
    y_send,
    y_in,
    z_edge,
    x_in,
    copy_sem,
    store_sem,
    send_sem,
    recv_sem,
):
    slabs, columns, layers, points, size_x, size_y = sizes
    ranks = columns * layers
    padded = blade.shape[0] // 3
    rows = 3 * padded
    capacity = point_in.shape[1]
    plane = size_x * size_y
    gx = lax.axis_index("gx")
    gy = lax.axis_index("gy")
    gz = lax.axis_index("gz")
    rank = gy * layers + gz
    inflow = inflow_values()

    loads = {}
    for number, (name, src, dst) in enumerate(
        (
            ("pops", pops_hbm, pops),
            ("count", count_hbm, count_in),
            ("owner", owner_hbm, owner_in),
            ("point", point_hbm, point_in),
            ("offset", offset_hbm, offset_in),
            ("weight", weight_hbm, weight_in),
            ("vel", vel_hbm, vel_in),
            ("rigid", rigid_hbm, rigid_in),
            ("drag", drag_hbm, drag_in),
            ("shapes", shapes_hbm, shapes),
            ("relax", relax_hbm, relax),
            ("disp", disp_hbm, disp_in),
            ("coupling", coupling_hbm, coupling),
        )
    ):
        loads[name] = pltpu.make_async_copy(src, dst, copy_sem.at[number])
        loads[name].start()

    def slab_peer(step):
        return lax.rem(rank + step, ranks)

    def slab_id(other):
        return (gx, lax.div(other, layers), lax.rem(other, layers))

    def far_id(step):
        return (lax.rem(gx + step, slabs), gy, gz)

    barrier = pltpu.get_barrier_semaphore()
    for step in range(1, slabs):
        pl.semaphore_signal(barrier, inc=1, device_id=far_id(step), device_id_type=MESH)
    for step in range(1, ranks):
        pl.semaphore_signal(
            barrier, inc=1, device_id=slab_id(slab_peer(step)), device_id_type=MESH
        )

    stores = []

    def store(src, dst):
        copy = pltpu.make_async_copy(src, dst, store_sem.at[len(stores)])
        copy.start()
        stores.append(copy)

    used = [0]
    started = []

    def send(src, dst, device):
        copy = pltpu.make_async_remote_copy(
            src_ref=src,
            dst_ref=dst,
            send_sem=send_sem.at[used[0]],
            recv_sem=recv_sem.at[used[0]],
            device_id=device,
            device_id_type=MESH,
        )
        used[0] += 1
        copy.start()
        started.append(copy)
        return copy

    loads["pops"].wait()

    def moments_of(step, _):
        part = pl.ds(pl.multiple_of(step * 8, 8), 8)
        values = transform([pops[i, part, :] for i in range(27)], to_moments)
        for m in range(27):
            moments[m, part, :] = values[m]
        inverse = 1.0 / values[0]
        for c, m in enumerate((9, 3, 1)):
            raw = values[m] * inverse
            spot = pl.ds(pl.multiple_of(step * 8 + c * plane, 8), 8)
            spread[spot, :] = raw
        return 0

    lax.fori_loop(0, plane // 8, moments_of, 0, unroll=2)
    raw_high, raw_low = halves(spread[...])
    raw_pair[:, :LANES] = raw_high
    raw_pair[:, LANES:] = raw_low

    for name in ("count", "owner", "point", "offset", "weight"):
        loads[name].wait()
    dense[...] = jnp.zeros_like(dense)
    count = count_in[0]
    iota_y = lax.broadcasted_iota(jnp.int32, (size_y, CHUNK), 0)
    iota_z = lax.broadcasted_iota(jnp.int32, (LANES, CHUNK), 0)
    iota_s = lax.broadcasted_iota(jnp.int32, (padded, CHUNK), 0)
    iota_r = lax.broadcasted_iota(jnp.int32, (1, CHUNK), 1)

    def slots_of(part):
        name = point_in[:, part]
        turbine = jnp.zeros_like(name)
        for t in range(1, slabs):
            turbine = turbine + jnp.where(name >= t * points, 1, 0)
        owner = jnp.zeros_like(name)
        for t in range(slabs):
            owner = owner + jnp.where(turbine == t, owner_in[t], 0)
        point = name - turbine * points
        high = lax.shift_right_logical(point, 7)
        masks = [(iota_s == owner) & (high == jh) for jh in range(8)]
        return point - high * LANES, masks

    def gather(step, _):
        base = pl.multiple_of(step * CHUNK, CHUNK)
        part = pl.ds(base, CHUNK)
        weight = jnp.where(iota_r + base < count, weight_in[:, part], 0.0)
        off_x = offset_in[0:1, part]
        off_y = offset_in[1:2, part]
        off_z = offset_in[2:3, part]
        at_y = [off_y + b == iota_y for b in range(TILE_SIDE)]
        by_x = []
        for x in range(size_x):
            value = jnp.zeros((16, CHUNK), jnp.float32)
            for a in range(TILE_SIDE):
                value = jnp.where(off_x + a == x, weight[16 * a : 16 * a + 16], value)
            by_x.append(value)
        total = [jnp.zeros((size_y, CHUNK), jnp.float32) for _ in range(3)]
        for c in range(TILE_SIDE):
            at_z = jnp.where(off_z + c == iota_z, 1.0, 0.0).astype(jnp.bfloat16)
            pick_z[c, :, part] = at_z
            layer = lax.dot_general(
                raw_pair[...],
                jnp.concatenate([at_z, at_z], axis=0),
                NN,
                preferred_element_type=jnp.float32,
            )
            for x in range(size_x):
                value = jnp.zeros((size_y, CHUNK), jnp.float32)
                for b in range(TILE_SIDE):
                    row = 4 * b + c
                    value = jnp.where(at_y[b], by_x[x][row : row + 1], value)
                kern_xy[c, x * size_y : (x + 1) * size_y, part] = value
                for d in range(3):
                    first = d * plane + x * size_y
                    total[d] = total[d] + value * layer[first : first + size_y]
        partial = [jnp.sum(t, axis=0, keepdims=True) for t in total]
        low, masks = slots_of(part)
        at_low = jnp.where(low == iota_z, 1.0, 0.0).astype(jnp.bfloat16)
        pick_low[:, part] = at_low
        placed = jnp.concatenate(
            [jnp.where(masks[jh], partial[d], 0.0) for jh in range(8) for d in range(3)], axis=0
        )
        high_part, low_part = halves(placed)
        dense[...] += (
            lax.dot_general(high_part, at_low, NT, preferred_element_type=jnp.float32)
            + lax.dot_general(low_part, at_low, NT, preferred_element_type=jnp.float32)
        ).reshape(8, rows, LANES)
        return 0

    lax.fori_loop(0, capacity // CHUNK, gather, 0, unroll=True)

    pl.semaphore_wait(barrier, slabs - 1 + ranks - 1)

    first_copies = [
        send(dense.at[slab_peer(step)], dense_in.at[step - 1], slab_id(slab_peer(step)))
        for step in range(1, ranks)
    ]
    for name in ("vel", "rigid", "drag", "shapes"):
        loads[name].wait()
    aux_in[...] = jnp.zeros_like(aux_in)
    for d in range(3):
        aux_in[d : d + 1, :points] = rigid_in[d]
    aux_in[3:4, :points] = drag_in[...]
    vel8 = jnp.broadcast_to(vel_in[...], (8, vel_in.shape[1])).astype(jnp.bfloat16)
    erow[...] = jnp.zeros_like(erow)
    erow[:, : 3 * points] = lax.dot_general(
        vel8, shapes[...], NT, preferred_element_type=jnp.float32
    )
    width = erow.shape[1]
    line = erow[...]
    shifted = [
        line if c == 0 else pltpu.roll(line, width - c * points, 1) for c in range(3)
    ]
    row8 = lax.broadcasted_iota(jnp.int32, (8, LANES), 0)
    lane8 = lax.broadcasted_iota(jnp.int32, (8, LANES), 1)
    for jh in range(8):
        spot = slice(jh * LANES, (jh + 1) * LANES)
        both = jnp.where(
            row8 == 0,
            shifted[0][:, spot],
            jnp.where(row8 == 1, shifted[1][:, spot], shifted[2][:, spot]),
        )
        inside = (row8 < 3) & (lane8 + jh * LANES < points)
        aux[jh] = aux_in[:, spot] + jnp.where(inside, both, 0.0)
    aux_copies = [
        send(aux.at[rank], aux_all.at[gx], far_id(step)) for step in range(1, slabs)
    ]
    aux_all[gx] = aux[rank]

    own = dense[rank]
    for step in range(1, ranks):
        first_copies[step - 1].wait_recv()
        own = own + dense_in[step - 1]
    slab_sum[...] = own
    second_copies = [
        send(slab_sum, slab_in.at[step - 1], far_id(step)) for step in range(1, slabs)
    ]
    for copy in aux_copies:
        copy.wait_recv()
    for step in range(1, slabs):
        second_copies[step - 1].wait_recv()
        own = own + slab_in[step - 1]

    blade[...] = jnp.zeros_like(blade)
    for s in range(slabs):
        here = aux_all[s]
        relative = [
            own[d * padded + s : d * padded + s + 1] - here[d : d + 1] for d in range(3)
        ]
        speed = jnp.sqrt(
            relative[0] * relative[0] + relative[1] * relative[1] + relative[2] * relative[2]
        )
        factor = here[3:4] * speed
        for d in range(3):
            spot = d * padded + s
            blade[spot : spot + 1, :] = factor * relative[d]
    blade_all[rank] = blade[...]
    third_copies = [
        send(blade, blade_all.at[rank], slab_id(slab_peer(step))) for step in range(1, ranks)
    ]
    for copy in third_copies:
        copy.wait_recv()

    blade_high, blade_low = halves(blade_all[...].reshape(8 * rows, LANES))
    blade_pair = jnp.concatenate([blade_high, blade_low], axis=1)
    spread[...] = jnp.zeros_like(spread)

    def scatter(step, _):
        part = pl.ds(pl.multiple_of(step * CHUNK, CHUNK), CHUNK)
        _, masks = slots_of(part)
        at_low = pick_low[:, part]
        found = lax.dot_general(
            blade_pair,
            jnp.concatenate([at_low, at_low], axis=0),
            NN,
            preferred_element_type=jnp.float32,
        )
        forces = []
        for d in range(3):
            value = jnp.zeros((padded, CHUNK), jnp.float32)
            for jh in range(8):
                first = jh * rows + d * padded
                value = jnp.where(masks[jh], found[first : first + padded], value)
            forces.append(jnp.sum(value, axis=0, keepdims=True))
        total = jnp.zeros(spread.shape, jnp.float32)
        for c in range(TILE_SIDE):
            kern = kern_xy[c, :, part]
            weighted = jnp.concatenate(
                [(kern * forces[d]).astype(jnp.bfloat16) for d in range(3)], axis=0
            )
            total = total + lax.dot_general(
                weighted, pick_z[c, :, part], NT, preferred_element_type=jnp.float32
            )
        spread[...] += total
        return 0

    lax.fori_loop(0, capacity // CHUNK, scatter, 0, unroll=True)
    force_out[...] = -spread[...]
    store(force_out, force_hbm_out)

    loads["relax"].wait()

    def collide(step, _):
        part = pl.ds(pl.multiple_of(step * 8, 8), 8)
        density = moments[0, part, :]
        inverse = 1.0 / density
        force = [
            force_unit * force_out[pl.ds(pl.multiple_of(step * 8 + d * plane, 8), 8), :]
            for d in range(3)
        ]
        velocity = [
            (moments[m, part, :] + 0.5 * force[d]) * inverse for d, m in enumerate((9, 3, 1))
        ]
        pushed = [density * v for v in velocity]
        pairs = {}
        sources = {}
        for d in range(3):
            for e in range(d, 3):
                pairs[d, e] = pushed[d] * velocity[e]
                sources[d, e] = velocity[d] * force[e] + velocity[e] * force[d]
        values = []
        for m in range(27):
            powers = (m // 9, m // 3 % 3, m % 3)
            odd = [d for d in range(3) if powers[d] == 1]
            even = [d for d in range(3) if powers[d] == 2]
            scale = (1.0 / 3.0) ** len(even)
            source = None
            if len(odd) == 0:
                wanted = density * scale
                if even:
                    square = pairs[even[0], even[0]]
                    source = sources[even[0], even[0]]
                    for d in even[1:]:
                        square = square + pairs[d, d]
                        source = source + sources[d, d]
                    wanted = wanted + square * (3.0 * scale)
                    source = source * (3.0 * scale)
            elif len(odd) == 1:
                wanted = pushed[odd[0]] * scale
                source = force[odd[0]] * scale
            elif len(odd) == 2:
                wanted = pairs[odd[0], odd[1]] * scale
                source = sources[odd[0], odd[1]] * scale
            else:
                wanted = None
            rate = relax[m]
            here = moments[m, part, :]
            gap = here if wanted is None else here - wanted
            value = -rate * gap
            if source is not None:
                value = value + (1.0 - 0.5 * rate) * source
            values.append(value)
        values = transform(values, from_moments)
        for i in range(27):
            cells[i, part, :] = pops[i, part, :] + values[i]
        return 0

    lax.fori_loop(0, plane // 8, collide, 0, unroll=2)

    lane = lax.broadcasted_iota(jnp.int32, (plane, LANES), 1)
    at_bottom = gz == 0
    packed = jnp.zeros((plane, LANES), jnp.float32)
    for k in range(9):
        column = jnp.where(
            at_bottom,
            pltpu.roll(cells[3 * k + 2], k + 1, 1),
            cells[3 * k] if k == 0 else pltpu.roll(cells[3 * k], k, 1),
        )
        packed = jnp.where(lane == k, column, packed)
    z_send[...] = packed
    next_y = lax.rem(gy + 1, columns)
    past_y = lax.rem(gy + columns - 1, columns)
    edge_copies = [
        send(z_send, z_in.at[0], (gx, gy, 1 - gz)),
        send(z_send, z_in.at[1], (gx, next_y, 1 - gz)),
        send(z_send, z_in.at[2], (gx, past_y, 1 - gz)),
    ]
    ups = [i for i in range(27) if i // 3 % 3 == 2]
    downs = [i for i in range(27) if i // 3 % 3 == 0]
    for k in range(9):
        for x in range(size_x):
            last = (x + 1) * size_y - 1
            y_send[0, k, x : x + 1, :] = cells[ups[k], last : last + 1, :]
            first = x * size_y
            y_send[1, k, x : x + 1, :] = cells[downs[k], first : first + 1, :]
    edge_copies += [
        send(y_send.at[0], y_in.at[0], (gx, next_y, gz)),
        send(y_send.at[1], y_in.at[1], (gx, past_y, gz)),
    ]
    for k in range(9):
        cells[3 * k + 2] = pltpu.roll(cells[3 * k + 2], 1, 1)
        cells[3 * k] = pltpu.roll(cells[3 * k], LANES - 1, 1)

    pieces = []
    for d in range(3):
        chunks = [
            jnp.broadcast_to(blade_all[jh, pl.ds(d * padded + gx, 1), :], (8, LANES))
            for jh in range(8)
        ]
        chunks.append(jnp.zeros((8, width - 8 * LANES), jnp.float32))
        piece = jnp.concatenate(chunks, axis=1)
        pieces.append(piece if d == 0 else pltpu.roll(piece, d * points, 1))
    erow[...] = pieces[0] + pieces[1] + pieces[2]
    modal = lax.dot_general(
        erow[:, : 3 * points].astype(jnp.bfloat16),
        shapes[...],
        NN,
        preferred_element_type=jnp.float32,
    )[0:1]
    loads["disp"].wait()
    loads["coupling"].wait()
    disp8 = jnp.broadcast_to(disp_in[...], (8, disp_in.shape[1]))
    stiff = lax.dot_general(
        disp8, coupling[...], NT, precision=highest, preferred_element_type=jnp.float32
    )[0:1]
    vel_new = vel_in[...] + modal_step * (modal - stiff)
    vel_out[...] = vel_new
    disp_out[...] = disp_in[...] + modal_step * vel_new
    store(vel_out, vel_hbm_out)
    store(disp_out, disp_hbm_out)

    def fill_lanes(k, side, column, rolled, lanes):
        if side == 2:
            above = column if k == 0 else pltpu.roll(column, LANES - k, 1)
            return jnp.where(
                lanes == 0, jnp.where(at_bottom, inflow[3 * k + 2], above), rolled
            )
        below = pltpu.roll(column, LANES - 1 - k, 1)
        return jnp.where(
            lanes == LANES - 1, jnp.where(at_bottom, below, inflow[3 * k]), rolled
        )

    for copy in edge_copies:
        copy.wait_recv()
    column = z_in[0]
    for k in range(9):
        for side in (0, 2):
            i = 3 * k + side
            cells[i] = fill_lanes(k, side, column, cells[i], lane)

    row = lax.broadcasted_iota(jnp.int32, (size_y, LANES), 0)
    z_edge[...] = jnp.zeros_like(z_edge)
    for x in range(size_x):
        last = (x + 1) * size_y - 1
        z_edge[0, x : x + 1, :] = z_in[1, last : last + 1, :]
        z_edge[1, x : x + 1, :] = z_in[2, x * size_y : x * size_y + 1, :]
    at_front, at_back = gy == 0, gy == columns - 1
    for k in range(9):
        for way, i in ((0, ups[k]), (1, downs[k])):
            halo = y_in[way, k]
            side = i % 3
            if side == 2:
                halo = fill_lanes(i // 3, 2, z_edge[way], pltpu.roll(halo, 1, 1), lane8)
            elif side == 0:
                halo = fill_lanes(i // 3, 0, z_edge[way], pltpu.roll(halo, LANES - 1, 1), lane8)
            halo = jnp.where(at_back if way else at_front, inflow[i], halo)
            for x in range(size_x):
                span = slice(x * size_y, (x + 1) * size_y)
                moved = pltpu.roll(cells[i, span, :], size_y - 1 if way else 1, 0)
                edge = size_y - 1 if way else 0
                cells[i, span, :] = jnp.where(row == edge, halo[x : x + 1], moved)

    tail = plane - size_y
    x_copies = [
        send(cells.at[pl.ds(18, 9), pl.ds(tail, size_y)], x_in.at[0], far_id(1)),
        send(cells.at[pl.ds(0, 9), pl.ds(0, size_y)], x_in.at[1], far_id(slabs - 1)),
    ]
    low, mid, high = (pl.ds(i, 9) for i in (0, 9, 18))
    inner, outer = pl.ds(0, tail), pl.ds(size_y, tail)
    first, last = pl.ds(0, size_y), pl.ds(tail, size_y)
    store(cells.at[mid], pops_hbm_out.at[mid])
    store(cells.at[high, inner], pops_hbm_out.at[high, outer])
    store(cells.at[low, outer], pops_hbm_out.at[low, inner])
    x_copies[0].wait_recv()
    store(x_in.at[0], pops_hbm_out.at[high, first])
    x_copies[1].wait_recv()
    store(x_in.at[1], pops_hbm_out.at[low, last])
    for copy in stores:
        copy.wait()
    for copy in started:
        copy.wait_send()


def store_kernel(*refs):
    sources, targets, held = refs[0:4], refs[4:8], refs[8:12]
    load_sem, store_sem = refs[12:]
    parts = [(0, pl.ds(i, 9)) for i in (9, 18, 0)] + [(k, slice(None)) for k in (1, 2, 3)]
    loads, stores = [], []
    for number, (k, part) in enumerate(parts):
        here = held[k].at[part]
        loads.append(pltpu.make_async_copy(sources[k].at[part], here, load_sem.at[number]))
        stores.append(pltpu.make_async_copy(here, targets[k].at[part], store_sem.at[number]))
        loads[-1].start()
    for load, store in zip(loads, stores):
        load.wait()
        store.start()
    for store in stores:
        store.wait()


def body(
    sizes,
    populations,
    relax,
    entry_point,
    entry_offset,
    entry_weight,
    entry_count,
    turbine_owner,
    mode_shapes,
    coupling,
    modal_disp,
    modal_vel,
    rigid_vel,
    drag_coef,
):
    slabs, columns, layers = sizes
    _, size_x, size_y, size_z = populations.shape
    points = drag_coef.shape[1]
    modes = modal_vel.shape[1]
    capacity = entry_point.shape[0]
    plane = size_x * size_y
    padded = -(-slabs // 8) * 8
    rows = 3 * padded
    ranks = columns * layers
    width = -(-3 * points // LANES) * LANES
    assert ranks == 8 and layers == 2 and size_z == LANES and points <= 8 * LANES
    assert columns > 2 and size_x <= 8
    copies = 2 * (slabs - 1) + 2 * (ranks - 1) + 7
    hbm = pl.BlockSpec(memory_space=pltpu.HBM)
    whole = jnp.int32
    full = jnp.float32
    half = jnp.bfloat16
    out = pl.pallas_call(
        functools.partial(kernel, (slabs, columns, layers, points, size_x, size_y)),
        out_shape=(
            jax.ShapeDtypeStruct((27, plane, size_z), full),
            jax.ShapeDtypeStruct((3 * plane, size_z), full),
            jax.ShapeDtypeStruct((1, modes), full),
            jax.ShapeDtypeStruct((1, modes), full),
        ),
        in_specs=[hbm] * 13,
        out_specs=(hbm,) * 4,
        scratch_shapes=[
            pltpu.VMEM((3 * plane, size_z), full),
            pltpu.VMEM((1, modes), full),
            pltpu.VMEM((1, modes), full),
            pltpu.VMEM((27, plane, size_z), full),
            pltpu.SMEM(relax.shape, full),
            pltpu.VMEM((1, capacity), whole),
            pltpu.VMEM(entry_offset.shape, whole),
            pltpu.VMEM(entry_weight.shape, full),
            pltpu.SMEM(entry_count.shape, whole),
            pltpu.SMEM(turbine_owner.shape, whole),
            pltpu.VMEM((3 * points, modes), half),
            pltpu.VMEM((modes, modes), full),
            pltpu.VMEM((1, modes), full),
            pltpu.VMEM((1, modes), full),
            pltpu.VMEM((3, 1, points), full),
            pltpu.VMEM((1, points), full),
            pltpu.VMEM((8, 8 * LANES), full),
            pltpu.VMEM((27, plane, size_z), full),
            pltpu.VMEM((27, plane, size_z), full),
            pltpu.VMEM((3 * plane, 2 * LANES), half),
            pltpu.VMEM((TILE_SIDE, LANES, capacity), half),
            pltpu.VMEM((TILE_SIDE, plane, capacity), full),
            pltpu.VMEM((LANES, capacity), half),
            pltpu.VMEM((8, rows, LANES), full),
            pltpu.VMEM((ranks - 1, rows, LANES), full),
            pltpu.VMEM((rows, LANES), full),
            pltpu.VMEM((slabs - 1, rows, LANES), full),
            pltpu.VMEM((8, 8, LANES), full),
            pltpu.VMEM((slabs, 8, LANES), full),
            pltpu.VMEM((rows, LANES), full),
            pltpu.VMEM((8, rows, LANES), full),
            pltpu.VMEM((8, width), full),
            pltpu.VMEM((3 * plane, LANES), full),
            pltpu.VMEM((plane, LANES), full),
            pltpu.VMEM((3, plane, LANES), full),
            pltpu.VMEM((2, 9, 8, LANES), full),
            pltpu.VMEM((2, 9, 8, LANES), full),
            pltpu.VMEM((2, 8, LANES), full),
            pltpu.VMEM((2, 9, size_y, LANES), full),
            pltpu.SemaphoreType.DMA((13,)),
            pltpu.SemaphoreType.DMA((8,)),
            pltpu.SemaphoreType.DMA((copies,)),
            pltpu.SemaphoreType.DMA((copies,)),
        ],
        compiler_params=pltpu.CompilerParams(
            collective_id=0, has_side_effects=True, vmem_limit_bytes=VMEM_BYTES
        ),
    )(
        populations.reshape(27, plane, size_z),
        relax,
        entry_point[None, :],
        entry_offset,
        entry_weight,
        entry_count,
        turbine_owner,
        mode_shapes[0],
        coupling[0],
        modal_disp,
        modal_vel,
        rigid_vel.transpose(1, 0, 2),
        drag_coef,
    )
    populations_out, body_force, disp_new, vel_new = pl.pallas_call(
        store_kernel,
        out_shape=tuple(jax.ShapeDtypeStruct(o.shape, o.dtype) for o in out),
        in_specs=[hbm] * 4,
        out_specs=(hbm,) * 4,
        scratch_shapes=[pltpu.VMEM(o.shape, o.dtype) for o in out]
        + [pltpu.SemaphoreType.DMA((6,))] * 2,
        compiler_params=pltpu.CompilerParams(
            has_side_effects=True, vmem_limit_bytes=VMEM_BYTES
        ),
    )(*out)
    return (
        populations_out.reshape(populations.shape),
        body_force.reshape(3, size_x, size_y, size_z),
        disp_new,
        vel_new,
    )


def solution(mesh):
    sizes = (mesh.shape["gx"], mesh.shape["gy"], mesh.shape["gz"])
    return jax.shard_map(
        functools.partial(body, sizes),
        mesh=mesh,
        in_specs=(
            P(None, "gx", "gy", "gz"),
            P(),
            P(("gx", "gy", "gz")),
            P(None, ("gx", "gy", "gz")),
            P(None, ("gx", "gy", "gz")),
            P(("gx", "gy", "gz")),
            P(),
            P("gx", None, None),
            P("gx", None, None),
            P("gx", None),
            P("gx", None),
            P("gx", None, None),
            P("gx", None),
        ),
        out_specs=(
            P(None, "gx", "gy", "gz"),
            P(None, "gx", "gy", "gz"),
            P("gx", None),
            P("gx", None),
        ),
        check_vma=False,
    )
```
